256 devices in a mesh: grp: 4 (over x_hi, core), vocab: 64 (over z, x_lo, y).
Axes of the slice: x: 4 (x_hi: 2, x_lo: 2; x = x_hi * 2 + x_lo), y: 4, z: 8, core: 2. Of those that a mesh axis runs over, the one named last changes fastest.
Arguments:
- hidden: bfloat16 [512, 3584], P('grp'), may hold values from -300 to 300
- token_ids: int32 [512], P('grp'), may hold values from 0 to 131071
- serving: int32 [512], replicated, may hold values from 0 to 511, each once
- head_weight: bfloat16 [3584, 131072], P(None, ('grp', 'vocab')), may hold values from -0.3125 to 0.3125
- teacher_logits: bfloat16 [512, 4, 32768], P('grp', None, 'vocab'), may hold values from -300 to 300
Outputs:
- grad_hidden: float32 [512, 3584], P(('grp', 'vocab'))
- grad_head: bfloat16 [3584, 131072], P(None, ('grp', 'vocab'))
The draws below stay inside these ranges and needn't reach their ends.
All inputs are finite; a program needn't handle non-finite values.
Results may differ from the reference program's by a relative error of at most 0.012.
Values may be sent and summed in bfloat16 or wider, within the bound.
A program may use at most 128 MiB of HBM per device.

```python
import math
import jax
import jax.numpy as jnp
import numpy as np
from jax import lax

DS = 3584
VOCAB_DEV = 512
GRPS = 4
ROWS_ALL = 512
VOCAB = 131072
VQ = 32768
N_VOCAB = 64


def shared_directions(key):
    return jax.random.normal(jax.random.fold_in(key, 5), (3, DS), jnp.float32) / math.sqrt(DS)


def draw_hidden(key, part):
    directions = shared_directions(key)
    key = jax.random.fold_in(key, 11)
    key_base, key_scale, key_load = jax.random.split(key, 3)
    scales = jnp.exp(jax.random.uniform(key_scale, (ROWS_ALL, 1), jnp.float32, math.log(0.5), math.log(5.0)))
    loads = 2.0 * jax.random.normal(key_load, (ROWS_ALL, 3), jnp.float32)
    along = loads[:, 0:1] * directions[0][None, :] + loads[:, 1:2] * directions[1][None, :] + loads[:, 2:3] * directions[2][None, :]
    base = jax.random.normal(key_base, (ROWS_ALL, DS), jnp.float32)
    values = jnp.clip((base + along) * scales, -30.0, 30.0)
    return values.astype(jnp.bfloat16)


def draw_head_weight(key, part):
    directions = shared_directions(key)
    key = jax.random.fold_in(key, 37)
    key_noise, key_center, key_coef = jax.random.split(key, 3)
    unit = 3.0 / math.sqrt(DS)
    coefs = jax.random.normal(key_coef, (3, VOCAB), jnp.float32)
    noise = jax.random.normal(key_noise, (DS, VOCAB), jnp.float32)
    center = jax.random.normal(key_center, (DS, 1), jnp.float32)
    values = unit * (noise + center) + directions[0][:, None] * coefs[0][None, :] + directions[1][:, None] * coefs[1][None, :] + directions[2][:, None] * coefs[2][None, :]
    return jnp.clip(values, -0.3125, 0.3125).astype(jnp.bfloat16)


def draw_teacher_logits(key, part):
    key = jax.random.fold_in(key, 23)
    key_base, key_scale = jax.random.split(key)
    scales = jnp.exp(jax.random.uniform(key_scale, (ROWS_ALL, 1, 1), jnp.float32, 0.0, math.log(3.0)))
    base = jax.random.normal(key_base, (ROWS_ALL, GRPS, VQ), jnp.float32)
    values = jnp.clip(base * 3.0 * scales, -40.0, 40.0)
    return values.astype(jnp.bfloat16)


def with_ends(result, rng, least, largest):
    place = [jax.random.randint(jax.random.fold_in(rng, axis), (), 0, length) for axis, length in enumerate(result.shape)]
    main_axis = result.shape.index(max(result.shape))
    beside = place[:main_axis] + [(place[main_axis] + 1) % result.shape[main_axis]] + place[main_axis + 1:]
    return result.at[tuple(place)].set(least).at[tuple(beside)].set(largest)


def wide_ids(own_key, dims, number_of, skew):
    weights = [min(1 << octave, number_of + 1 - (1 << octave)) * (1 << 20) // math.isqrt((1 << octave) ** skew) + 1 for octave in range((number_of + 1).bit_length()) if 1 << octave <= number_of]
    spread = 1 + sum(weights) // (1 << 30)
    grid = np.cumsum(np.array([max(1, weight // spread) for weight in weights]))
    ticket = jax.random.randint(jax.random.fold_in(own_key, 1), dims, 0, int(grid[len(weights) - 1]))
    start = jnp.left_shift(1, jnp.searchsorted(jnp.asarray(grid, jnp.int32), ticket, side="right").astype(jnp.int32))
    rank = start - 1 + jax.random.randint(jax.random.fold_in(own_key, 4), dims, 0, 1 << 30) % jnp.minimum(start, number_of + 1 - start)
    return jax.random.permutation(jax.random.fold_in(own_key, 2), number_of)[rank].astype(jnp.int32)


def setup_inputs(seed: int = 0) -> dict:
    arg_keys = jax.random.split(jax.random.key(seed), 6)
    hidden = draw_hidden(jax.random.fold_in(arg_keys[5], 71), 0)
    token_ids = with_ends(wide_ids(arg_keys[1], (ROWS_ALL,), VOCAB, 2), jax.random.fold_in(arg_keys[1], 3), 0, VOCAB - 1).astype(jnp.int32)
    serving = jax.random.permutation(arg_keys[2], ROWS_ALL).astype(jnp.int32)
    head_weight = draw_head_weight(jax.random.fold_in(arg_keys[5], 71), 0)
    teacher_logits = draw_teacher_logits(jax.random.fold_in(arg_keys[5], 71), 0)
    return dict(hidden=hidden, token_ids=token_ids, serving=serving, head_weight=head_weight, teacher_logits=teacher_logits)


smoothing_divisor = 2.0
imitation_mixing_coefficient = 0.5
objective_scaling_factor = 32.0


def reference(hidden, token_ids, serving, head_weight, teacher_logits):
    rows_all = hidden.shape[0]
    mentor_activations = teacher_logits.reshape(rows_all, VOCAB)[serving].astype(jnp.float32)
    logits = jnp.dot(hidden, head_weight, preferred_element_type=jnp.float32)
    student_peak = jnp.max(logits, axis=1, keepdims=True)
    mentor_peak_activation = jnp.max(mentor_activations, axis=1, keepdims=True)
    shifted_pupil_activations = logits - student_peak
    mentor_shifted_activations = (mentor_activations - mentor_peak_activation) / smoothing_divisor
    sum_hard = jnp.sum(jnp.exp(shifted_pupil_activations), axis=1, keepdims=True)
    mentor_component_accumulated = jnp.sum(jnp.exp(shifted_pupil_activations / smoothing_divisor), axis=1, keepdims=True)
    mentor_exponential_summed = jnp.sum(jnp.exp(mentor_shifted_activations), axis=1, keepdims=True)
    columns = jnp.arange(VOCAB, dtype=jnp.int32)
    labels = (token_ids[:, None] == columns[None, :]).astype(jnp.float32)
    mentor_match_component = jnp.exp(shifted_pupil_activations / smoothing_divisor) / mentor_component_accumulated - jnp.exp(mentor_shifted_activations) / mentor_exponential_summed
    ground_truth_component = jnp.exp(shifted_pupil_activations) / sum_hard - labels
    activation_derivative = (objective_scaling_factor * (imitation_mixing_coefficient * smoothing_divisor * mentor_match_component + (1.0 - imitation_mixing_coefficient) * ground_truth_component)).astype(jnp.bfloat16)
    grad_hidden = lax.dot_general(activation_derivative, head_weight, (((1,), (1,)), ((), ())), preferred_element_type=jnp.float32)
    blocks = GRPS * N_VOCAB
    grad_blocks = activation_derivative.reshape(rows_all, blocks, VOCAB_DEV).transpose(1, 0, 2)
    hidden_t = hidden.T

    def one_block(block):
        return jnp.dot(hidden_t, block, preferred_element_type=jnp.float32).astype(jnp.bfloat16)

    grad_head = lax.map(one_block, grad_blocks).transpose(1, 0, 2).reshape(DS, VOCAB)
    return grad_hidden, grad_head
```

```python
import functools

import jax
import jax.numpy as jnp
from jax import lax
from jax.experimental import pallas as pl
from jax.experimental.pallas import tpu as pltpu
from jax.sharding import PartitionSpec as P

MESH = pl.DeviceIdType.MESH
F32 = jnp.float32
BF16 = jnp.bfloat16
I32 = jnp.int32

DS = 3584
COLS = 512
GRPS = 4
ROWS = 512
GROWS = 128
NX, NY, NZ = 4, 4, 8

Y0 = 384
Y1 = 256
ZW = 128
YB1 = NY * Y0
ZB = YB1 + NY * Y1

NCH = 4
CW = DS // NCH

HCH = 7
HW = DS // HCH


def device(x, y, z, c):
    return (lax.div(x, 2) * 2 + c, (z * 2 + lax.rem(x, 2)) * 4 + y)


def merge(blocks):
    ms = functools.reduce(jnp.maximum, [b[0:1] for b in blocks])
    mt = functools.reduce(jnp.maximum, [b[1:2] for b in blocks])
    hard = soft = teach = 0.0
    for b in blocks:
        d = jnp.exp((b[0:1] - ms) * 0.5)
        hard = hard + b[2:3] * (d * d)
        soft = soft + b[3:4] * d
        teach = teach + b[4:5] * jnp.exp((b[1:2] - mt) * 0.5)
    return ms, mt, hard, soft, teach


def kernel(
    hid, ids, srv, w_hbm, t_hbm, gh_out, ghead_out,
    h_all, w, wt, ht, tv, tst, tall, ids_all, pt, perm, lg, et, stc, st, st_c, st_x, st_y, st_z, fin, fint,
    g, gp, own, dsend, drecv, s1, r1, acc, s2, r2, s3, r3, gheadv,
    ssem, rsem, lsem,
):
    gi = lax.axis_index("grp")
    vi = lax.axis_index("vocab")
    c = lax.rem(gi, 2)
    xh = lax.div(gi, 2)
    y = lax.rem(vi, 4)
    xl = lax.rem(lax.div(vi, 4), 2)
    z = lax.div(vi, 8)
    x = 2 * xh + xl
    other = device(x, y, z, 1 - c)
    partner = device(3 - x, y, z, c)
    xs = [device(lax.rem(x + k, NX), y, z, c) for k in range(1, NX)]
    ys = [device(x, lax.rem(y + k, NY), z, c) for k in range(1, NY)]
    zs = [device(x, y, lax.rem(z + k, NZ), c) for k in range(1, NZ)]
    far = device(lax.rem(x + 2, NX), y, z, 1 - c)

    bar = pltpu.get_barrier_semaphore()
    peers = [other, *xs, *ys, *zs, far]
    for p in peers:
        pl.semaphore_signal(bar, inc=1, device_id=p, device_id_type=MESH)

    count = [0]
    started = []

    def send(src, dst, to):
        k = count[0]
        count[0] += 1
        cp = pltpu.make_async_remote_copy(
            src_ref=src, dst_ref=dst, send_sem=ssem.at[k], recv_sem=rsem.at[k], device_id=to, device_id_type=MESH
        )
        cp.start()
        started.append(cp)
        return cp

    load_t = pltpu.make_async_copy(t_hbm, tv, lsem.at[0])
    load_t.start()
    load_h = pltpu.make_async_copy(hid, h_all.at[gi], lsem.at[1])
    load_h.start()
    load_w = pltpu.make_async_copy(w_hbm, w, lsem.at[2])
    load_w.start()

    pt[...] = (lax.broadcasted_iota(I32, (ROWS, ROWS), 0) == srv[...]).astype(BF16)
    ids_all[gi] = ids[...]
    load_t.wait()
    for q in range(GRPS):
        tst[q] = tv[:, q, :]

    pl.semaphore_wait(bar, len(peers))

    def zcols(k):
        return pl.ds(pl.multiple_of(ZB + k * ZW, ZW), ZW)

    def ycols(j, k):
        base, width = ((0, Y0), (YB1, Y1))[j]
        return pl.ds(pl.multiple_of(base + k * width, 128), width)

    cross_z = send(hid.at[:, zcols(z)], h_all.at[gi, :, zcols(z)], partner)
    cross_y = [send(hid.at[:, ycols(j, y)], h_all.at[gi, :, ycols(j, y)], partner) for j in range(2)]
    pair = send(hid, h_all.at[gi], other)
    teach, idc = [], []
    for k in range(1, GRPS):
        q = lax.rem(gi + k, GRPS)
        to = (q, vi)
        idc.append(send(ids_all.at[gi], ids_all.at[gi], to))
        teach.append(send(tst.at[q], tall.at[gi], to))
    tall[gi] = tst[gi]

    gg = 2 * (1 - xh) + c
    cross_z.wait_recv()
    fwd_z = [send(h_all.at[gg, :, zcols(z)], h_all.at[gg, :, zcols(z)], p) for p in zs]
    fwd_y = []
    for j in range(2):
        cross_y[j].wait_recv()
        fwd_y.append([send(h_all.at[gg, :, ycols(j, y)], h_all.at[gg, :, ycols(j, y)], p) for p in ys])

    load_w.wait()
    load_h.wait()
    pair.wait_recv()

    def logits(half):
        row = pl.multiple_of(half * 256, 256)
        for j in range(2):
            a = h_all[2 * half + j]
            lg[pl.ds(pl.multiple_of(row + j * 128, 128), 128), :] = jnp.dot(a, w[...], preferred_element_type=F32)

    logits(xh)

    def turn_rows(half):
        for j in range(2):
            gr = 2 * half + j

            def step(i, _):
                s = pl.ds(pl.multiple_of(i * HW, HW), HW)
                ht[s, pl.ds(pl.multiple_of(gr * GROWS, GROWS), GROWS)] = h_all[gr, :, s].T
                return 0

            lax.fori_loop(0, HCH, step, 0)

    def student_stats(half):
        def step(j, _):
            r = pl.ds(pl.multiple_of(half * 256 + j * 128, 128), 128)
            l = lg[r, :]
            m = jnp.max(l, axis=1, keepdims=True)
            e = jnp.exp((l - m) * 0.5)
            lg[r, :] = e
            lane = lax.broadcasted_iota(I32, (128, 128), 1)
            hard = jnp.sum(e * e, axis=1, keepdims=True)
            soft = jnp.sum(e, axis=1, keepdims=True)
            stc[r, :] = jnp.where(lane == 0, m, jnp.where(lane == 2, hard, jnp.where(lane == 3, soft, stc[r, :])))
            return 0

        lax.fori_loop(0, 2, step, 0)

    def share(refs):
        return [send(h_all.at[gg, :, s], h_all.at[gg, :, s], other) for s in refs]

    for cp in fwd_z:
        cp.wait_recv()
    shared = share([pl.ds(ZB, NZ * ZW)])
    for cp in fwd_y[0]:
        cp.wait_recv()
    shared += share([pl.ds(0, YB1)])

    for cp in teach:
        cp.wait_recv()
    al = lax.dot_general(
        pt[...], tall[...].reshape(ROWS, COLS), (((0,), (0,)), ((), ())), preferred_element_type=F32
    )
    et[...] = al

    def teacher_stats(j, _):
        r = pl.ds(pl.multiple_of(j * 128, 128), 128)
        a = et[r, :]
        m = jnp.max(a, axis=1, keepdims=True)
        e = jnp.exp((a - m) * 0.5)
        et[r, :] = e
        lane = lax.broadcasted_iota(I32, (128, 128), 1)
        stc[r, :] = jnp.where(lane == 1, m, jnp.where(lane == 4, jnp.sum(e, axis=1, keepdims=True), 0.0))
        return 0

    lax.fori_loop(0, 4, teacher_stats, 0)

    for cp in fwd_y[1]:
        cp.wait_recv()
    shared += share([pl.ds(YB1, NY * Y1)])
    student_stats(xh)

    for cp in shared:
        cp.wait_recv()
    logits(1 - xh)
    student_stats(1 - xh)

    def put(ref, stats):
        for k, s in enumerate(stats):
            ref[k : k + 1, :] = s

    for j in range(4):
        st[0, :, j * 128 : (j + 1) * 128] = stc[j * 128 : (j + 1) * 128, :].T[0:8, :]
    cp = send(st.at[0], st_c, other)
    turn_rows(xh)
    cp.wait_recv()
    put(st.at[1], merge([st[0], st_c[...]]))
    cps = [send(st.at[1], st_x.at[k], p) for k, p in enumerate(xs)]
    turn_rows(1 - xh)
    for cp in cps:
        cp.wait_recv()
    put(st.at[2], merge([st[1], *[st_x[k] for k in range(NX - 1)]]))
    cps = [send(st.at[2], st_y.at[k], p) for k, p in enumerate(ys)]

    def turn_w(i, _):
        s = pl.ds(pl.multiple_of(i * HW, HW), HW)
        wt[:, s] = w[s, :].T
        return 0

    lax.fori_loop(0, HCH, turn_w, 0)
    for cp in cps:
        cp.wait_recv()
    put(st.at[3], merge([st[2], *[st_y[k] for k in range(NY - 1)]]))
    cps = [send(st.at[3], st_z.at[k], p) for k, p in enumerate(zs)]

    i = lax.broadcasted_iota(I32, (ROWS, 1), 0)
    i_c, i_x, i_y = lax.div(i, 256), lax.rem(lax.div(i, 64), 4), lax.rem(lax.div(i, 16), 4)
    i_z, i_b = lax.rem(lax.div(i, 2), 8), lax.rem(i, 2)
    r = (2 * lax.div(i_x, 2) + i_c) * 128 + i_z * 16 + lax.rem(i_x, 2) * 8 + i_y * 2 + i_b
    perm[...] = (lax.broadcasted_iota(I32, (ROWS, ROWS), 1) == r).astype(BF16)
    for cp in idc:
        cp.wait_recv()

    for cp in cps:
        cp.wait_recv()
    ms, mt, hard, soft, teach_sum = merge([st[3], *[st_z[k] for k in range(NZ - 1)]])
    d = jnp.exp((st[0, 0:1, :] - ms) * 0.5)
    fin[...] = jnp.zeros_like(fin)
    fin[0:1, :] = 32.0 * d / soft
    fin[1:2, :] = 32.0 * jnp.exp((st[0, 1:2, :] - mt) * 0.5) / teach_sum
    fin[2:3, :] = 16.0 * d * d / hard
    for j in range(4):
        fin[3:4, j * 128 : (j + 1) * 128] = ids_all[j].astype(F32)
    for j in range(4):
        fint[j * 128 : (j + 1) * 128, :] = fin[:, j * 128 : (j + 1) * 128].T

    first = (gi * (NX // 2 * NY * NZ) + vi) * COLS

    def grad(j, _):
        r = pl.ds(pl.multiple_of(j * 128, 128), 128)
        f = fint[r, :]
        e = lg[r, :]
        col = lax.broadcasted_iota(I32, (128, COLS), 1) + first
        hit = jnp.where(f[:, 3:4].astype(I32) == col, 16.0, 0.0)
        g[r, :] = (e * f[:, 0:1] - et[r, :] * f[:, 1:2] + (e * e * f[:, 2:3] - hit)).astype(BF16)
        return 0

    lax.fori_loop(0, 4, grad, 0)
    gp[...] = jnp.dot(perm[...], g[...], preferred_element_type=F32).astype(BF16)

    pairs, ones, twos = [], [], []

    def first_stage(ch):
        pairs[ch].wait_recv()

        def step(k, _):
            s1[ch, k] = (own[ch, k] + drecv[ch, k].astype(F32)).astype(BF16)
            return 0

        lax.fori_loop(0, NX, step, 0)
        if ch % 2 == 0:
            ones.append([send(s1.at[ch, lax.rem(x + k, NX)], r1.at[ch, k - 1], p) for k, p in enumerate(xs, 1)])
        else:
            ones.append([send(s1.at[ch, :, lax.rem(y + k, NY)], r1.at[ch, k - 1], p) for k, p in enumerate(ys, 1)])

    def half_rows(k):
        return gp[pl.ds(pl.multiple_of(k * 256, 256), 256), :]

    for ch in range(NCH):
        s = slice(ch * CW, (ch + 1) * CW)
        dsend[ch] = (
            jnp.dot(half_rows(1 - c), wt[:, s], preferred_element_type=F32).astype(BF16).reshape(NX, NY, 16, CW)
        )
        pairs.append(send(dsend.at[ch], drecv.at[ch], other))
        own[ch] = jnp.dot(half_rows(c), wt[:, s], preferred_element_type=F32).reshape(NX, NY, 16, CW)
        if ch:
            first_stage(ch - 1)
    first_stage(NCH - 1)

    stores = []

    def head(k):
        s = pl.ds(k * HW, HW)
        gheadv[s, :] = jnp.dot(ht[s, :], g[...], preferred_element_type=F32).astype(BF16)
        cp = pltpu.make_async_copy(gheadv.at[s], ghead_out.at[s], lsem.at[3 + k])
        cp.start()
        stores.append(cp)

    heads = list(range(HCH))

    def second_stage(ch):
        for cp in ones[ch]:
            cp.wait_recv()
        for j in range(4):
            place = (ch, x, j) if ch % 2 == 0 else (ch, j, y)
            t = own[place] + drecv[place].astype(F32)
            for k in range(3):
                t = t + r1[ch, k, j].astype(F32)
            acc[ch, j] = t
            s2[ch, j] = t.astype(BF16)
        n, me, to = (NY, y, ys) if ch % 2 == 0 else (NX, x, xs)
        twos.append([send(s2.at[ch, lax.rem(me + k, n)], r2.at[ch, k - 1], p) for k, p in enumerate(to, 1)])

    for ch in range(NCH):
        for _ in range(2):
            if heads:
                head(heads.pop(0))
        second_stage(ch)
    while heads:
        head(heads.pop(0))

    for ch in range(NCH):
        for cp in twos[ch]:
            cp.wait_recv()
        t = acc[ch, y if ch % 2 == 0 else x]
        for k in range(3):
            t = t + r2[ch, k].astype(F32)
        for j in range(NZ):
            s3[j, :, ch * CW : (ch + 1) * CW] = t[2 * j : 2 * j + 2, :]
    threes = [send(s3.at[lax.rem(z + k, NZ)], r3.at[k - 1], p) for k, p in enumerate(zs, 1)]
    for cp in threes:
        cp.wait_recv()
    t = s3[z]
    for k in range(NZ - 1):
        t = t + r3[k]
    gh_out[...] = t

    for cp in started:
        cp.wait_send()
    for cp in stores:
        cp.wait()


N_SEMS = 96


def body(hidden, token_ids, serving, head_weight, teacher_logits):
    vm = pltpu.VMEM
    return pl.pallas_call(
        kernel,
        out_shape=(
            jax.ShapeDtypeStruct((2, DS), F32),
            jax.ShapeDtypeStruct((DS, COLS), BF16),
        ),
        in_specs=[
            pl.BlockSpec(memory_space=pl.ANY),
            pl.BlockSpec(memory_space=vm),
            pl.BlockSpec(memory_space=vm),
            pl.BlockSpec(memory_space=pl.ANY),
            pl.BlockSpec(memory_space=pl.ANY),
        ],
        out_specs=(pl.BlockSpec(memory_space=vm), pl.BlockSpec(memory_space=pl.ANY)),
        scratch_shapes=[
            vm((GRPS, GROWS, DS), BF16),
            vm((DS, COLS), BF16),
            vm((COLS, DS), BF16),
            vm((DS, ROWS), BF16),
            vm((GROWS, GRPS, COLS), BF16),
            vm((GRPS, GROWS, COLS), BF16),
            vm((GRPS, GROWS, COLS), BF16),
            vm((GRPS, 1, GROWS), I32),
            vm((ROWS, ROWS), BF16),
            vm((ROWS, ROWS), BF16),
            vm((ROWS, COLS), F32),
            vm((ROWS, COLS), F32),
            vm((ROWS, 128), F32),
            vm((4, 8, ROWS), F32),
            vm((8, ROWS), F32),
            vm((NX - 1, 8, ROWS), F32),
            vm((NY - 1, 8, ROWS), F32),
            vm((NZ - 1, 8, ROWS), F32),
            vm((128, ROWS), F32),
            vm((ROWS, 128), F32),
            vm((ROWS, COLS), BF16),
            vm((ROWS, COLS), BF16),
            vm((NCH, NX, NY, 16, CW), F32),
            vm((NCH, NX, NY, 16, CW), BF16),
            vm((NCH, NX, NY, 16, CW), BF16),
            vm((NCH, NX, NY, 16, CW), BF16),
            vm((NCH, 3, 4, 16, CW), BF16),
            vm((NCH, 4, 16, CW), F32),
            vm((NCH, 4, 16, CW), BF16),
            vm((NCH, 3, 16, CW), BF16),
            vm((NZ, 2, DS), F32),
            vm((NZ - 1, 2, DS), F32),
            vm((DS, COLS), BF16),
            pltpu.SemaphoreType.DMA((N_SEMS,)),
            pltpu.SemaphoreType.DMA((N_SEMS,)),
            pltpu.SemaphoreType.DMA((3 + HCH,)),
        ],
        compiler_params=pltpu.CompilerParams(
            collective_id=0, has_side_effects=True, vmem_limit_bytes=60 * 1024 * 1024
        ),
        name="distill_backward",
    )(hidden, token_ids.reshape(1, GROWS), serving.reshape(1, ROWS), head_weight, teacher_logits)


def solution(mesh):
    placed = (P("grp", None), P("grp"), P(), P(None, ("grp", "vocab")), P("grp", None, "vocab"))
    return jax.shard_map(
        body,
        mesh=mesh,
        in_specs=placed,
        out_specs=(P(("grp", "vocab"), None), P(None, ("grp", "vocab"))),
        check_vma=False,
    )
```

```python
import functools

import jax
import jax.numpy as jnp
from jax import lax
from jax.experimental import pallas as pl
from jax.experimental.pallas import tpu as pltpu
from jax.sharding import PartitionSpec as P

MESH = pl.DeviceIdType.MESH
F32 = jnp.float32
BF16 = jnp.bfloat16
I32 = jnp.int32

DS = 3584
COLS = 512
GRPS = 4
ROWS = 512
GROWS = 128
NX, NY, NZ = 4, 4, 8

Y0 = 384
Y1 = 256
ZW = 128
YB1 = NY * Y0
ZB = YB1 + NY * Y1

NCH = 4
CW = DS // NCH

HCH = 7
HW = DS // HCH


def device(x, y, z, c):
    return (lax.div(x, 2) * 2 + c, (z * 2 + lax.rem(x, 2)) * 4 + y)


def merge(blocks):
    ms = functools.reduce(jnp.maximum, [b[0:1] for b in blocks])
    mt = functools.reduce(jnp.maximum, [b[3:4] for b in blocks])
    hard = soft = teach = 0.0
    for b in blocks:
        d = jnp.exp((b[0:1] - ms) * 0.5)
        hard = hard + b[1:2] * (d * d)
        soft = soft + b[2:3] * d
        teach = teach + jnp.exp(b[3:4] - mt)
    return ms, hard, soft, mt + jnp.log(teach)


def kernel(
    hid, ids_hbm, srv_hbm, w_hbm, t_hbm, gh_out, ghead_out,
    ids, srv, h_all, w, wt, ht, tv, tst, tall, ids_all, pt, perm, lg, et, stc, st, st_c, st_x, st_y, st_z, fin, fint,
    g, gp, own, dsend, drecv, s1, r1, acc, s2, r2, acc3, s3f, s3, r3,
    ssem, rsem, lsem,
):
    gi = lax.axis_index("grp")
    vi = lax.axis_index("vocab")
    c = lax.rem(gi, 2)
    xh = lax.div(gi, 2)
    y = lax.rem(vi, 4)
    xl = lax.rem(lax.div(vi, 4), 2)
    z = lax.div(vi, 8)
    x = 2 * xh + xl
    other = device(x, y, z, 1 - c)
    partner = device(3 - x, y, z, c)
    xs = [device(lax.rem(x + k, NX), y, z, c) for k in range(1, NX)]
    ys = [device(x, lax.rem(y + k, NY), z, c) for k in range(1, NY)]
    zs = [device(x, y, lax.rem(z + k, NZ), c) for k in range(1, NZ)]
    far = device(lax.rem(x + 2, NX), y, z, 1 - c)

    bar = pltpu.get_barrier_semaphore()
    peers = [other, *xs, *ys, *zs, far]
    for p in peers:
        pl.semaphore_signal(bar, inc=1, device_id=p, device_id_type=MESH)

    count = [0]
    started = []

    def send(src, dst, to):
        k = count[0]
        count[0] += 1
        cp = pltpu.make_async_remote_copy(
            src_ref=src, dst_ref=dst, send_sem=ssem.at[k], recv_sem=rsem.at[k], device_id=to, device_id_type=MESH
        )
        cp.start()
        started.append(cp)
        return cp

    load_s = [pltpu.make_async_copy(ids_hbm, ids, lsem.at[3]), pltpu.make_async_copy(srv_hbm, srv, lsem.at[4])]
    for cp in load_s:
        cp.start()
    load_t = pltpu.make_async_copy(t_hbm, tv, lsem.at[0])
    load_t.start()
    load_h = pltpu.make_async_copy(hid, h_all.at[gi], lsem.at[1])
    load_h.start()
    load_w = pltpu.make_async_copy(w_hbm, w, lsem.at[2])
    load_w.start()

    for cp in load_s:
        cp.wait()
    pt[...] = (lax.broadcasted_iota(I32, (ROWS, ROWS), 0) == srv[...]).astype(BF16)
    ids_all[gi] = ids[...]
    pl.semaphore_wait(bar, len(peers))

    def zcols(k):
        return pl.ds(pl.multiple_of(ZB + k * ZW, ZW), ZW)

    def ycols(j, k):
        base, width = ((0, Y0), (YB1, Y1))[j]
        return pl.ds(pl.multiple_of(base + k * width, 128), width)

    cross_z = send(hid.at[:, zcols(z)], h_all.at[gi, :, zcols(z)], partner)
    cross_y = [send(hid.at[:, ycols(j, y)], h_all.at[gi, :, ycols(j, y)], partner) for j in range(2)]
    pair = send(hid, h_all.at[gi], other)
    idc = [send(ids_all.at[gi], ids_all.at[gi], (lax.rem(gi + k, GRPS), vi)) for k in range(1, GRPS)]

    load_t.wait()
    for q in range(GRPS):
        tst[q] = tv[:, q, :]
    t_all = tst[...].astype(F32)
    tm = jnp.max(jnp.max(t_all, axis=0), axis=1, keepdims=True)
    tsum = jnp.sum(jnp.sum(jnp.exp((t_all - tm[None]) * 0.5), axis=0), axis=1, keepdims=True)
    lse = jnp.broadcast_to(tm * 0.5 + jnp.log(tsum), (GROWS, 128))
    st[0, 3:4, :] = jnp.full((1, ROWS), -1e30, F32)
    st[0, 3:4, pl.ds(pl.multiple_of(gi * GROWS, GROWS), GROWS)] = lse.T[0:1, :]

    gg = 2 * (1 - xh) + c
    cross_z.wait_recv()
    fwd_z = [send(h_all.at[gg, :, zcols(z)], h_all.at[gg, :, zcols(z)], p) for p in zs]
    fwd_y = []
    for j in range(2):
        cross_y[j].wait_recv()
        fwd_y.append([send(h_all.at[gg, :, ycols(j, y)], h_all.at[gg, :, ycols(j, y)], p) for p in ys])

    teach = []
    for k in range(1, GRPS):
        q = lax.rem(gi + k, GRPS)
        teach.append(send(tst.at[q], tall.at[gi], (q, vi)))
    tall[gi] = tst[gi]

    load_w.wait()
    load_h.wait()
    pair.wait_recv()

    def logits(half):
        row = pl.multiple_of(half * 256, 256)
        for j in range(2):
            a = h_all[2 * half + j]
            lg[pl.ds(pl.multiple_of(row + j * 128, 128), 128), :] = jnp.dot(a, w[...], preferred_element_type=F32)

    logits(xh)

    def turn_rows(half):
        for j in range(2):
            gr = 2 * half + j

            def step(i, _):
                s = pl.ds(pl.multiple_of(i * HW, HW), HW)
                ht[s, pl.ds(pl.multiple_of(gr * GROWS, GROWS), GROWS)] = h_all[gr, :, s].T
                return 0

            lax.fori_loop(0, HCH, step, 0)

    def student_stats(half):
        def step(j, _):
            r = pl.ds(pl.multiple_of(half * 256 + j * 128, 128), 128)
            l = lg[r, :]
            m = jnp.max(l, axis=1, keepdims=True)
            e = jnp.exp((l - m) * 0.5)
            lg[r, :] = e
            lane = lax.broadcasted_iota(I32, (128, 128), 1)
            hard = jnp.sum(e * e, axis=1, keepdims=True)
            soft = jnp.sum(e, axis=1, keepdims=True)
            stc[r, :] = jnp.where(lane == 0, m, jnp.where(lane == 1, hard, soft))
            return 0

        lax.fori_loop(0, 2, step, 0)

    def share(refs):
        return [send(h_all.at[gg, :, s], h_all.at[gg, :, s], other) for s in refs]

    for cp in fwd_z:
        cp.wait_recv()
    shared = share([pl.ds(ZB, NZ * ZW)])
    for cp in fwd_y[0]:
        cp.wait_recv()
    shared += share([pl.ds(0, YB1)])

    for cp in fwd_y[1]:
        cp.wait_recv()
    shared += share([pl.ds(YB1, NY * Y1)])
    student_stats(xh)

    for cp in shared:
        cp.wait_recv()
    logits(1 - xh)
    student_stats(1 - xh)

    def put(ref, stats):
        for k, s in enumerate(stats):
            ref[k : k + 1, :] = s

    for j in range(4):
        st[0, 0:3, j * 128 : (j + 1) * 128] = stc[j * 128 : (j + 1) * 128, :].T[0:3, :]
    cp = send(st.at[0], st_c, other)
    turn_rows(xh)
    cp.wait_recv()
    put(st.at[1], merge([st[0], st_c[...]]))
    cps = [send(st.at[1], st_x.at[k], p) for k, p in enumerate(xs)]
    turn_rows(1 - xh)
    for cp in cps:
        cp.wait_recv()
    put(st.at[2], merge([st[1], *[st_x[k] for k in range(NX - 1)]]))
    cps = [send(st.at[2], st_y.at[k], p) for k, p in enumerate(ys)]

    def turn_w(i, _):
        s = pl.ds(pl.multiple_of(i * HW, HW), HW)
        wt[:, s] = w[s, :].T
        return 0

    lax.fori_loop(0, HCH, turn_w, 0)
    for cp in cps:
        cp.wait_recv()
    put(st.at[3], merge([st[2], *[st_y[k] for k in range(NY - 1)]]))
    cps = [send(st.at[3], st_z.at[k], p) for k, p in enumerate(zs)]

    i = lax.broadcasted_iota(I32, (ROWS, 1), 0)
    i_c, i_x, i_y = lax.div(i, 256), lax.rem(lax.div(i, 64), 4), lax.rem(lax.div(i, 16), 4)
    i_z, i_b = lax.rem(lax.div(i, 2), 8), lax.rem(i, 2)
    r = (2 * lax.div(i_x, 2) + i_c) * 128 + i_z * 16 + lax.rem(i_x, 2) * 8 + i_y * 2 + i_b
    perm[...] = (lax.broadcasted_iota(I32, (ROWS, ROWS), 1) == r).astype(BF16)
    for cp in idc:
        cp.wait_recv()
    for cp in teach:
        cp.wait_recv()
    et[...] = lax.dot_general(
        pt[...], tall[...].reshape(ROWS, COLS), (((0,), (0,)), ((), ())), preferred_element_type=F32
    )
    fin[...] = jnp.zeros_like(fin)
    for j in range(4):
        fin[2:3, j * 128 : (j + 1) * 128] = ids_all[j].astype(F32)

    for cp in cps:
        cp.wait_recv()
    ms, hard, soft, lse = merge([st[3], *[st_z[k] for k in range(NZ - 1)]])
    d = jnp.exp((st[0, 0:1, :] - ms) * 0.5)
    fin[0:1, :] = 32.0 * d / soft
    fin[1:2, :] = 16.0 * d * d / hard
    for k in range(3):
        term = lse.astype(BF16).astype(F32)
        fin[8 + k : 9 + k, :] = term
        lse = lse - term
    terms = jnp.dot(fin[8:16, :].astype(BF16), pt[...], preferred_element_type=F32)
    fin[3:4, :] = terms[0:1] + terms[1:2] + terms[2:3]
    for j in range(4):
        fint[j * 128 : (j + 1) * 128, :] = fin[:, j * 128 : (j + 1) * 128].T

    first = (gi * (NX // 2 * NY * NZ) + vi) * COLS

    def grad(j, _):
        r = pl.ds(pl.multiple_of(j * 128, 128), 128)
        f = fint[r, :]
        e = lg[r, :]
        col = lax.broadcasted_iota(I32, (128, COLS), 1) + first
        hit = jnp.where(f[:, 2:3].astype(I32) == col, 16.0, 0.0)
        soft = e * f[:, 0:1] - 32.0 * jnp.exp(et[r, :] * 0.5 - f[:, 3:4])
        g[r, :] = (soft + (e * e * f[:, 1:2] - hit)).astype(BF16)
        return 0

    lax.fori_loop(0, 4, grad, 0)
    gp[...] = jnp.dot(perm[...], g[...], preferred_element_type=F32).astype(BF16)

    pairs, ones, twos = [], [], []

    def first_stage(ch):
        pairs[ch].wait_recv()

        def step(k, _):
            s1[ch, k] = (own[ch, k] + drecv[ch, k].astype(F32)).astype(BF16)
            return 0

        lax.fori_loop(0, NX, step, 0)
        if ch % 2 == 0:
            ones.append([send(s1.at[ch, lax.rem(x + k, NX)], r1.at[ch, k - 1], p) for k, p in enumerate(xs, 1)])
        else:
            ones.append([send(s1.at[ch, :, lax.rem(y + k, NY)], r1.at[ch, k - 1], p) for k, p in enumerate(ys, 1)])

    def half_rows(k):
        return gp[pl.ds(pl.multiple_of(k * 256, 256), 256), :]

    for ch in range(NCH):
        s = slice(ch * CW, (ch + 1) * CW)
        dsend[ch] = (
            jnp.dot(half_rows(1 - c), wt[:, s], preferred_element_type=F32).astype(BF16).reshape(NX, NY, 16, CW)
        )
        pairs.append(send(dsend.at[ch], drecv.at[ch], other))
        own[ch] = jnp.dot(half_rows(c), wt[:, s], preferred_element_type=F32).reshape(NX, NY, 16, CW)
        if ch:
            first_stage(ch - 1)
    first_stage(NCH - 1)


    def head(k):
        s = pl.ds(k * HW, HW)
        ghead_out[s, :] = jnp.dot(ht[s, :], g[...], preferred_element_type=F32).astype(BF16)

    heads = list(range(HCH))

    def second_stage(ch):
        for cp in ones[ch]:
            cp.wait_recv()
        for j in range(4):
            place = (ch, x, j) if ch % 2 == 0 else (ch, j, y)
            t = own[place] + drecv[place].astype(F32)
            for k in range(3):
                t = t + r1[ch, k, j].astype(F32)
            acc[ch, j] = t
            s2[ch, j] = t.astype(BF16)
        n, me, to = (NY, y, ys) if ch % 2 == 0 else (NX, x, xs)
        twos.append([send(s2.at[ch, lax.rem(me + k, n)], r2.at[ch, k - 1], p) for k, p in enumerate(to, 1)])

    for ch in range(NCH):
        for _ in range(2):
            if heads:
                head(heads.pop(0))
        second_stage(ch)
    while heads:
        head(heads.pop(0))

    for ch in range(NCH):
        for cp in twos[ch]:
            cp.wait_recv()
        t = acc[ch, y if ch % 2 == 0 else x]
        for k in range(3):
            t = t + r2[ch, k].astype(F32)
        acc3[:, ch * CW : (ch + 1) * CW] = t
    s3f[:, 14:16, :] = jnp.zeros((NZ, 2, 512), F32)
    for j in range(NZ):
        for k in range(DS // 512):
            s3f[j, 2 * k : 2 * k + 2, :] = acc3[2 * j : 2 * j + 2, k * 512 : (k + 1) * 512]
    s3[...] = s3f[...].astype(BF16)
    threes = [send(s3.at[lax.rem(z + k, NZ)], r3.at[k - 1], p) for k, p in enumerate(zs, 1)]
    for cp in threes:
        cp.wait_recv()
    t = s3f[z]
    for k in range(NZ - 1):
        t = t + r3[k].astype(F32)
    for k in range(DS // 512):
        gh_out[:, k * 512 : (k + 1) * 512] = t[2 * k : 2 * k + 2, :]

    for cp in started:
        cp.wait_send()


def write_out(sums, head, gh_out, ghead_out, sem):
    cps = [pltpu.make_async_copy(sums, gh_out, sem.at[HCH])]
    for k in range(HCH):
        s = pl.ds(k * HW, HW)
        cps.append(pltpu.make_async_copy(head.at[s], ghead_out.at[s], sem.at[k]))
    for cp in cps:
        cp.start()
    for cp in cps:
        cp.wait()


N_SEMS = 96


def body(hidden, token_ids, serving, head_weight, teacher_logits):
    vm = pltpu.VMEM
    sums, head = pl.pallas_call(
        kernel,
        out_shape=(
            vm((2, DS), F32),
            vm((DS, COLS), BF16),
        ),
        in_specs=[pl.BlockSpec(memory_space=pltpu.HBM)] * 5,
        out_specs=(pl.BlockSpec(memory_space=vm), pl.BlockSpec(memory_space=vm)),
        scratch_shapes=[
            vm((1, GROWS), I32),
            vm((1, ROWS), I32),
            vm((GRPS, GROWS, DS), BF16),
            vm((DS, COLS), BF16),
            vm((COLS, DS), BF16),
            vm((DS, ROWS), BF16),
            vm((GROWS, GRPS, COLS), BF16),
            vm((GRPS, GROWS, COLS), BF16),
            vm((GRPS, GROWS, COLS), BF16),
            vm((GRPS, 1, GROWS), I32),
            vm((ROWS, ROWS), BF16),
            vm((ROWS, ROWS), BF16),
            vm((ROWS, COLS), F32),
            vm((ROWS, COLS), F32),
            vm((ROWS, 128), F32),
            vm((4, 4, ROWS), F32),
            vm((4, ROWS), F32),
            vm((NX - 1, 4, ROWS), F32),
            vm((NY - 1, 4, ROWS), F32),
            vm((NZ - 1, 4, ROWS), F32),
            vm((128, ROWS), F32),
            vm((ROWS, 128), F32),
            vm((ROWS, COLS), BF16),
            vm((ROWS, COLS), BF16),
            vm((NCH, NX, NY, 16, CW), F32),
            vm((NCH, NX, NY, 16, CW), BF16),
            vm((NCH, NX, NY, 16, CW), BF16),
            vm((NCH, NX, NY, 16, CW), BF16),
            vm((NCH, 3, 4, 16, CW), BF16),
            vm((NCH, 4, 16, CW), F32),
            vm((NCH, 4, 16, CW), BF16),
            vm((NCH, 3, 16, CW), BF16),
            vm((16, DS), F32),
            vm((NZ, 16, 512), F32),
            vm((NZ, 16, 512), BF16),
            vm((NZ - 1, 16, 512), BF16),
            pltpu.SemaphoreType.DMA((N_SEMS,)),
            pltpu.SemaphoreType.DMA((N_SEMS,)),
            pltpu.SemaphoreType.DMA((5,)),
        ],
        compiler_params=pltpu.CompilerParams(
            collective_id=0, has_side_effects=True, vmem_limit_bytes=48 * 1024 * 1024
        ),
        name="distill_backward",
    )(*[
        pltpu.with_memory_space_constraint(a, pltpu.HBM)
        for a in (hidden, token_ids.reshape(1, GROWS), serving.reshape(1, ROWS), head_weight, teacher_logits)
    ])
    return pl.pallas_call(
        write_out,
        out_shape=(
            jax.ShapeDtypeStruct((2, DS), F32),
            jax.ShapeDtypeStruct((DS, COLS), BF16),
        ),
        in_specs=[pl.BlockSpec(memory_space=vm)] * 2,
        out_specs=(pl.BlockSpec(memory_space=pl.ANY), pl.BlockSpec(memory_space=pl.ANY)),
        scratch_shapes=[pltpu.SemaphoreType.DMA((1 + HCH,))],
        compiler_params=pltpu.CompilerParams(vmem_limit_bytes=1024 * 1024),
        name="write_out",
    )(sums, head)


def solution(mesh):
    placed = (P("grp", None), P("grp"), P(), P(None, ("grp", "vocab")), P("grp", None, "vocab"))
    return jax.shard_map(
        body,
        mesh=mesh,
        in_specs=placed,
        out_specs=(P(("grp", "vocab"), None), P(None, ("grp", "vocab"))),
        check_vma=False,
    )
```

```python
import functools

import jax
import jax.numpy as jnp
from jax import lax
from jax.experimental import pallas as pl
from jax.experimental.pallas import tpu as pltpu
from jax.sharding import PartitionSpec as P

MESH = pl.DeviceIdType.MESH
F32 = jnp.float32
BF16 = jnp.bfloat16
I32 = jnp.int32

DS = 3584
COLS = 512
GRPS = 4
ROWS = 512
GROWS = 128
NX, NY, NZ = 4, 4, 8

HROWS = GROWS // 2
HALF = ROWS // 2

YW = 640
ZW = 128
ZB = NY * YW

CW = DS // 2

HCH = 7
HW = DS // HCH


def device(x, y, z, c):
    return (lax.div(x, 2) * 2 + c, (z * 2 + lax.rem(x, 2)) * 4 + y)


def merge(blocks):
    ms = functools.reduce(jnp.maximum, [b[0:1] for b in blocks])
    hard = soft = 0.0
    for b in blocks:
        d = jnp.exp((b[0:1] - ms) * 0.5)
        hard = hard + b[1:2] * (d * d)
        soft = soft + b[2:3] * d
    if blocks[0].shape[0] == 4:
        return ms, hard, soft
    mt = functools.reduce(jnp.maximum, [b[3:5] for b in blocks])
    teach = 0.0
    for b in blocks:
        teach = teach + jnp.exp(b[3:5] - mt)
    return ms, hard, soft, mt + jnp.log(teach)


def put(ref, stats):
    k = 0
    for s in stats:
        ref[k : k + s.shape[0], :] = s
        k += s.shape[0]


def kernel(
    hid, ids_hbm, srv_hbm, w_hbm, t_hbm, gh_out, ghead_out,
    ids, srv, h_all, w, wt, ht, tv, tst, tall, ids_all, pt, perm, lg, al, stc,
    sta, sta_c, sta_x, sta_y, sta_z, stb, stb_c, stb_x, stb_y, stb_z,
    fin, fint, rowf, rowt, g, gp, own, dsend, drecv, s1, r1, s1b, r1b, acc, s2, r2, acc3, s3f, s3, r3,
    ssem, rsem, lsem,
):
    gi = lax.axis_index("grp")
    vi = lax.axis_index("vocab")
    c = lax.rem(gi, 2)
    xh = lax.div(gi, 2)
    y = lax.rem(vi, 4)
    xl = lax.rem(lax.div(vi, 4), 2)
    z = lax.div(vi, 8)
    x = 2 * xh + xl
    other = device(x, y, z, 1 - c)
    partner = device(3 - x, y, z, c)
    xs = [device(lax.rem(x + k, NX), y, z, c) for k in range(1, NX)]
    ys = [device(x, lax.rem(y + k, NY), z, c) for k in range(1, NY)]
    zs = [device(x, y, lax.rem(z + k, NZ), c) for k in range(1, NZ)]
    far = device(lax.rem(x + 2, NX), y, z, 1 - c)

    bar = pltpu.get_barrier_semaphore()
    peers = [other, *xs, *ys, *zs, far]
    for p in peers:
        pl.semaphore_signal(bar, inc=1, device_id=p, device_id_type=MESH)

    count = [0]
    started = []

    def send(src, dst, to):
        k = count[0]
        count[0] += 1
        cp = pltpu.make_async_remote_copy(
            src_ref=src, dst_ref=dst, send_sem=ssem.at[k], recv_sem=rsem.at[k], device_id=to, device_id_type=MESH
        )
        cp.start()
        started.append(cp)
        return cp

    def load(src, dst, k):
        cp = pltpu.make_async_copy(src, dst, lsem.at[k])
        cp.start()
        return cp

    def await_all(cps):
        for cp in cps:
            cp.wait_recv()

    def rows_of(h):
        return pl.ds(h * HROWS, HROWS)

    load_ids = load(ids_hbm, ids, 0)
    load_srv = load(srv_hbm, srv, 1)
    load_t = load(t_hbm, tv, 2)
    load_h = [load(hid.at[rows_of(h)], h_all.at[h, gi], 3 + h) for h in range(2)]
    load_w = load(w_hbm, w, 5)

    load_ids.wait()
    load_srv.wait()
    pt[...] = (lax.broadcasted_iota(I32, (ROWS, ROWS), 0) == srv[...]).astype(BF16)
    ids_all[gi] = ids[...]
    for cp in load_h:
        cp.wait()

    pl.semaphore_wait(bar, len(peers))

    ycols = pl.ds(pl.multiple_of(y * YW, 128), YW)
    zcols = pl.ds(pl.multiple_of(ZB + z * ZW, ZW), ZW)
    cross_y, cross_z = [], []
    for h in range(2):
        for cols, cps in ((zcols, cross_z), (ycols, cross_y)):
            piece = h_all.at[h, gi, :, cols]
            cps.append(send(piece, piece, partner))
    pair = [send(h_all.at[h, gi], h_all.at[h, gi], other) for h in range(2)]
    idc = [send(ids_all.at[gi], ids_all.at[gi], (lax.rem(gi + k, GRPS), vi)) for k in range(1, GRPS)]

    load_t.wait()
    for q in range(GRPS):
        tst[q] = tv[:, q, :]
    t_all = tst[...].astype(F32)
    tm = jnp.max(jnp.max(t_all, axis=0), axis=1, keepdims=True)
    tsum = jnp.sum(jnp.sum(jnp.exp((t_all - tm[None]) * 0.5), axis=0), axis=1, keepdims=True)
    lse = jnp.broadcast_to(tm * 0.5 + jnp.log(tsum), (GROWS, 128)).T[0:1, :]
    none = jnp.full((1, GROWS), -1e30, F32)
    for j in range(GRPS):
        sta[0, 3 + j // 2 : 4 + j // 2, (j % 2) * GROWS : (j % 2 + 1) * GROWS] = jnp.where(gi == j, lse, none)

    gg = 2 * (1 - xh) + c
    fwd_y, fwd_z = [], []

    def forward(h):
        cross_z[h].wait_recv()
        piece = h_all.at[h, gg, :, zcols]
        fwd_z.append([send(piece, piece, p) for p in zs])
        cross_y[h].wait_recv()
        piece = h_all.at[h, gg, :, ycols]
        fwd_y.append([send(piece, piece, p) for p in ys])

    def share(h):
        cps = []
        for fwd, cols in ((fwd_y, pl.ds(0, ZB)), (fwd_z, pl.ds(ZB, NZ * ZW))):
            await_all(fwd[h])
            piece = h_all.at[h, gg, :, cols]
            cps.append(send(piece, piece, other))
        return cps

    def two_groups(part):
        return pl.ds(pl.multiple_of(part * GROWS, GROWS), GROWS)

    def logits(h, part):
        a = h_all[h, pl.ds(2 * part, 2)].reshape(GROWS, DS)
        lg[h, two_groups(part), :] = jnp.dot(a, w[...], preferred_element_type=F32)

    def student_stats(h, part):
        r = two_groups(part)
        l = lg[h, r, :]
        m = jnp.max(l, axis=1, keepdims=True)
        e = jnp.exp((l - m) * 0.5)
        lg[h, r, :] = e
        lane = lax.broadcasted_iota(I32, (GROWS, 128), 1)
        hard = jnp.sum(e * e, axis=1, keepdims=True)
        soft = jnp.sum(e, axis=1, keepdims=True)
        stc[h, r, :] = jnp.where(lane == 0, m, jnp.where(lane == 1, hard, soft))

    def turn_rows(h, part):
        cols = pl.ds(pl.multiple_of(h * HALF + part * GROWS, GROWS), GROWS)

        def step(i, _):
            s = pl.ds(pl.multiple_of(i * HW, HW), HW)
            ht[s, cols] = h_all[h, pl.ds(2 * part, 2), :, s].reshape(GROWS, HW).T
            return 0

        lax.fori_loop(0, HCH, step, 0)

    forward(0)
    load_w.wait()
    await_all(pair)
    logits(0, xh)
    forward(1)
    teach = []
    for k in range(1, GRPS):
        q = lax.rem(gi + k, GRPS)
        teach.append(send(tst.at[q], tall.at[gi], (q, vi)))
    tall[gi] = tst[gi]
    logits(1, xh)
    student_stats(0, xh)

    st = [sta, stb]
    st_c = [sta_c, stb_c]
    st_x = [sta_x, stb_x]
    st_y = [sta_y, stb_y]
    st_z = [sta_z, stb_z]

    def stats_begin(h):
        for j in range(2):
            s = slice(j * 128, (j + 1) * 128)
            st[h][0, 0:3, s] = stc[h, s, :].T[0:3, :]
        return [send(st[h].at[0], st_c[h], other)]

    def stats_x(h, cps):
        await_all(cps)
        put(st[h].at[1], merge([st[h][0], st_c[h][...]]))
        return [send(st[h].at[1], st_x[h].at[k], p) for k, p in enumerate(xs)]

    def stats_y(h, cps):
        await_all(cps)
        put(st[h].at[2], merge([st[h][1], *[st_x[h][k] for k in range(NX - 1)]]))
        return [send(st[h].at[2], st_y[h].at[k], p) for k, p in enumerate(ys)]

    def stats_z(h, cps):
        await_all(cps)
        put(st[h].at[3], merge([st[h][2], *[st_y[h][k] for k in range(NY - 1)]]))
        return [send(st[h].at[3], st_z[h].at[k], p) for k, p in enumerate(zs)]

    def stats_end(h, cps):
        await_all(cps)
        ms, hard, soft, *lse = merge([st[h][3], *[st_z[h][k] for k in range(NZ - 1)]])
        d = jnp.exp((st[h][0, 0:1, :] - ms) * 0.5)
        fin[0:1, :] = 32.0 * d / soft
        fin[1:2, :] = 16.0 * d * d / hard
        for j in range(2):
            s = slice(j * 128, (j + 1) * 128)
            fint[h, s, :] = fin[:, s].T
        return lse

    def turn_w(first, last):
        def step(i, _):
            s = pl.ds(pl.multiple_of(i * HW, HW), HW)
            wt[:, s] = w[s, :].T
            return 0

        lax.fori_loop(first, last, step, 0)

    def make_perm():
        i = lax.broadcasted_iota(I32, (HALF, 1), 0)
        i_c, hi, lo = lax.div(i, 128), lax.rem(lax.div(i, 32), 4), lax.rem(lax.div(i, 8), 4)
        i_z, i_b = lax.rem(lax.div(i, 2), 4), lax.rem(i, 2)
        col = lax.broadcasted_iota(I32, (HALF, HALF), 1)
        for p, (i_x, i_y) in enumerate(((hi, lo), (lo, hi))):
            r = (2 * lax.div(i_x, 2) + i_c) * HROWS + i_z * 16 + lax.rem(i_x, 2) * 8 + i_y * 2 + i_b
            perm[p] = (col == r).astype(BF16)

    fin[...] = jnp.zeros_like(fin)
    rowf[...] = jnp.zeros_like(rowf)
    shared = [share(0)]
    student_stats(1, xh)
    await_all(shared[0])
    logits(0, 1 - xh)
    student_stats(0, 1 - xh)
    m0 = stats_begin(0)
    shared.append(share(1))
    m0 = stats_x(0, m0)
    await_all(shared[1])
    logits(1, 1 - xh)
    student_stats(1, 1 - xh)
    m1 = stats_begin(1)
    m0 = stats_y(0, m0)
    m1 = stats_x(1, m1)
    make_perm()
    turn_w(0, 3)
    m0 = stats_z(0, m0)
    m1 = stats_y(1, m1)
    turn_w(3, HCH)

    await_all(teach)
    al[...] = lax.dot_general(
        pt[...], tall[...].reshape(ROWS, COLS), (((0,), (0,)), ((), ())), preferred_element_type=F32
    )
    await_all(idc)
    for j in range(GRPS):
        rowf[0:1, j * 128 : (j + 1) * 128] = ids_all[j].astype(F32)
    (lse,) = stats_end(0, m0)
    terms = 0.0
    for j in range(2):
        part = lse[j : j + 1, :]
        for k in range(3):
            term = part.astype(BF16).astype(F32)
            rowf[8 + k : 9 + k, j * HALF : (j + 1) * HALF] = term
            part = part - term
    terms = jnp.dot(rowf[8:16, :].astype(BF16), pt[...], preferred_element_type=F32)
    rowf[1:2, :] = terms[0:1] + terms[1:2] + terms[2:3]
    for j in range(4):
        s = slice(j * 128, (j + 1) * 128)
        rowt[s, :] = rowf[:, s].T

    first = (gi * (NX // 2 * NY * NZ) + vi) * COLS

    def grad(h):
        def step(j, _):
            r = pl.ds(pl.multiple_of(j * HROWS, HROWS), HROWS)
            full = pl.ds(pl.multiple_of(j * GROWS + h * HROWS, HROWS), HROWS)
            f = fint[h, r, :]
            f2 = rowt[full, :]
            e = lg[h, r, :]
            col = lax.broadcasted_iota(I32, (HROWS, COLS), 1) + first
            hit = jnp.where(f2[:, 0:1].astype(I32) == col, 16.0, 0.0)
            soft = e * f[:, 0:1] - 32.0 * jnp.exp(al[full, :] * 0.5 - f2[:, 1:2])
            g[pl.ds(pl.multiple_of(h * HALF + j * HROWS, HROWS), HROWS), :] = (
                soft + (e * e * f[:, 1:2] - hit)
            ).astype(BF16)
            return 0

        lax.fori_loop(0, GRPS, step, 0)
        for p in range(2):
            gp[p] = jnp.dot(perm[p], g[h * HALF : (h + 1) * HALF, :], preferred_element_type=F32).astype(BF16)

    def pair_stage(h):
        cps = []
        for p in range(2):
            s = slice(p * CW, (p + 1) * CW)
            t = jnp.dot(gp[p, two_groups(1 - c), :], wt[:, s], preferred_element_type=F32)
            dsend[h, p] = t.astype(BF16).reshape(4, 32, CW)
            cps.append(send(dsend.at[h, p], drecv.at[h, p], other))
        for p in range(2):
            s = slice(p * CW, (p + 1) * CW)
            t = jnp.dot(gp[p, two_groups(c), :], wt[:, s], preferred_element_type=F32)
            own[h, p] = t.reshape(4, 32, CW)
        return cps

    x_side = 2 * xh + 1 - xl
    y_side = y + 1 - 2 * lax.rem(y, 2)
    axes = [
        (x, ((3 - x, partner), (x_side, device(x_side, y, z, c))), y, ys),
        (y, ((3 - y, device(x, 3 - y, z, c)), (y_side, device(x, y_side, z, c))), x, xs),
    ]
    subs = (slice(0, CW // 2), slice(CW // 2, CW))

    def chip_sum(h, p, k, cols):
        return own[h, p, k, :, cols] + drecv[h, p, k, :, cols].astype(F32)

    def first_stage(h, p, cp):
        cp.wait_recv()
        me, sides, _, _ = axes[p]
        opposite = lax.rem(me + 2, 4)
        cps = []
        for i, cols in enumerate(subs):
            place, to = sides[i]
            s1[h, p, i, 0] = chip_sum(h, p, place, cols).astype(BF16)
            s1[h, p, i, 1] = chip_sum(h, p, opposite, cols).astype(BF16)
            cps.append(send(s1.at[h, p, i], r1.at[h, p, i], to))
        return cps

    def first_stage_end(h, p, cps):
        sides = axes[p][1]
        out = []
        for i, cols in enumerate(subs):
            cps[i].wait_recv()
            place, to = sides[1 - i]
            s1b[h, p, i] = (chip_sum(h, p, place, cols) + r1[h, p, i, 1].astype(F32)).astype(BF16)
            out.append(send(s1b.at[h, p, i], r1b.at[h, p, i], to))
        return out

    def second_stage(h, p, cps):
        await_all(cps)
        me, _, me2, to = axes[p]
        t = [chip_sum(h, p, me, cols) + (r1[h, p, i, 0].astype(F32) + r1b[h, p, i].astype(F32)) for i, cols in enumerate(subs)]
        for j in range(4):
            r = slice(j * 8, (j + 1) * 8)
            acc[h, p, j, :, subs[0]] = t[0][r]
            acc[h, p, j, :, subs[1]] = t[1][r]
            s2[h, p, j] = jnp.concatenate([t[0][r], t[1][r]], axis=0).astype(BF16)
        return [send(s2.at[h, p, lax.rem(me2 + k, 4)], r2.at[h, p, k - 1], d) for k, d in enumerate(to, 1)]

    base3 = 100
    s3f[:, 14:16, :] = jnp.zeros((NZ, 2, 512), F32)

    def third_copy(k, to):
        return pltpu.make_async_remote_copy(
            src_ref=s3.at[to],
            dst_ref=r3.at[k - 1],
            send_sem=ssem.at[base3 + k],
            recv_sem=rsem.at[base3 + k],
            device_id=device(x, y, to, c),
            device_id_type=MESH,
        )

    def third_stage(h, parts):
        for p, cps in enumerate(parts):
            await_all(cps)
            t = acc[h, p, axes[p][2]]
            u = r2[h, p, 0].astype(F32) + r2[h, p, 1].astype(F32) + r2[h, p, 2].astype(F32)
            base = p * CW
            acc3[:, base : base + CW // 2] = t[:, : CW // 2] + u[0:8]
            acc3[:, base + CW // 2 : base + CW] = t[:, CW // 2 :] + u[8:16]
        for j in range(4):
            for k in range(DS // 512):
                s3f[4 * h + j, 2 * k : 2 * k + 2, :] = acc3[2 * j : 2 * j + 2, k * 512 : (k + 1) * 512]
            s3[4 * h + j] = s3f[4 * h + j].astype(BF16)
        for k in range(1, NZ):
            to = lax.rem(z + k, NZ)

            @pl.when(lax.div(to, 4) == h)
            def _():
                third_copy(k, to).start()

    def third_end():
        for k in range(1, NZ):
            third_copy(k, lax.rem(z + k, NZ)).wait_recv()
        t = s3f[z]
        for k in range(NZ - 1):
            t = t + r3[k].astype(F32)
        for k in range(DS // 512):
            gh_out[:, k * 512 : (k + 1) * 512] = t[2 * k : 2 * k + 2, :]
        for k in range(1, NZ):
            third_copy(k, lax.rem(z + k, NZ)).wait_send()

    def head(first, last):
        def step(k, _):
            s = pl.ds(pl.multiple_of(k * HW, HW), HW)
            ghead_out[s, :] = jnp.dot(ht[s, :], g[...], preferred_element_type=F32).astype(BF16)
            return 0

        lax.fori_loop(first, last, step, 0)

    grad(0)
    m1 = stats_z(1, m1)
    a0, b0 = pair_stage(0)
    a0 = first_stage(0, 0, a0)
    b0 = first_stage(0, 1, b0)
    stats_end(1, m1)
    grad(1)
    a1, b1 = pair_stage(1)
    a0 = first_stage_end(0, 0, a0)
    b0 = first_stage_end(0, 1, b0)
    a1 = first_stage(1, 0, a1)
    b1 = first_stage(1, 1, b1)
    for h in range(2):
        turn_rows(h, xh)
    a0 = second_stage(0, 0, a0)
    b0 = second_stage(0, 1, b0)
    a1 = first_stage_end(1, 0, a1)
    b1 = first_stage_end(1, 1, b1)
    for h in range(2):
        turn_rows(h, 1 - xh)
    head(0, 2)
    third_stage(0, (a0, b0))
    a1 = second_stage(1, 0, a1)
    b1 = second_stage(1, 1, b1)
    head(2, HCH)
    third_stage(1, (a1, b1))
    third_end()

    for cp in started:
        cp.wait_send()


def write_out(sums, head, gh_out, ghead_out, sem):
    cps = [pltpu.make_async_copy(sums, gh_out, sem.at[HCH])]
    for k in range(HCH):
        s = pl.ds(k * HW, HW)
        cps.append(pltpu.make_async_copy(head.at[s], ghead_out.at[s], sem.at[k]))
    for cp in cps:
        cp.start()
    for cp in cps:
        cp.wait()


N_SEMS = 112


def body(hidden, token_ids, serving, head_weight, teacher_logits):
    vm = pltpu.VMEM
    sums, head = pl.pallas_call(
        kernel,
        out_shape=(
            vm((2, DS), F32),
            vm((DS, COLS), BF16),
        ),
        in_specs=[pl.BlockSpec(memory_space=pltpu.HBM)] * 5,
        out_specs=(pl.BlockSpec(memory_space=vm), pl.BlockSpec(memory_space=vm)),
        scratch_shapes=[
            vm((1, GROWS), I32),
            vm((1, ROWS), I32),
            vm((2, GRPS, HROWS, DS), BF16),
            vm((DS, COLS), BF16),
            vm((COLS, DS), BF16),
            vm((DS, ROWS), BF16),
            vm((GROWS, GRPS, COLS), BF16),
            vm((GRPS, GROWS, COLS), BF16),
            vm((GRPS, GROWS, COLS), BF16),
            vm((GRPS, 1, GROWS), I32),
            vm((ROWS, ROWS), BF16),
            vm((2, HALF, HALF), BF16),
            vm((2, HALF, COLS), F32),
            vm((ROWS, COLS), F32),
            vm((2, HALF, 128), F32),
            vm((4, 8, HALF), F32),
            vm((8, HALF), F32),
            vm((NX - 1, 8, HALF), F32),
            vm((NY - 1, 8, HALF), F32),
            vm((NZ - 1, 8, HALF), F32),
            vm((4, 4, HALF), F32),
            vm((4, HALF), F32),
            vm((NX - 1, 4, HALF), F32),
            vm((NY - 1, 4, HALF), F32),
            vm((NZ - 1, 4, HALF), F32),
            vm((128, HALF), F32),
            vm((2, HALF, 128), F32),
            vm((128, ROWS), F32),
            vm((ROWS, 128), F32),
            vm((ROWS, COLS), BF16),
            vm((2, HALF, COLS), BF16),
            vm((2, 2, 4, 32, CW), F32),
            vm((2, 2, 4, 32, CW), BF16),
            vm((2, 2, 4, 32, CW), BF16),
            vm((2, 2, 2, 2, 32, CW // 2), BF16),
            vm((2, 2, 2, 2, 32, CW // 2), BF16),
            vm((2, 2, 2, 32, CW // 2), BF16),
            vm((2, 2, 2, 32, CW // 2), BF16),
            vm((2, 2, 4, 8, CW), F32),
            vm((2, 2, 4, 16, CW // 2), BF16),
            vm((2, 2, 3, 16, CW // 2), BF16),
            vm((8, DS), F32),
            vm((NZ, 16, 512), F32),
            vm((NZ, 16, 512), BF16),
            vm((NZ - 1, 16, 512), BF16),
            pltpu.SemaphoreType.DMA((N_SEMS,)),
            pltpu.SemaphoreType.DMA((N_SEMS,)),
            pltpu.SemaphoreType.DMA((6,)),
        ],
        compiler_params=pltpu.CompilerParams(
            collective_id=0, has_side_effects=True, vmem_limit_bytes=48 * 1024 * 1024
        ),
        name="distill_backward",
    )(*[
        pltpu.with_memory_space_constraint(a, pltpu.HBM)
        for a in (hidden, token_ids.reshape(1, GROWS), serving.reshape(1, ROWS), head_weight, teacher_logits)
    ])
    return pl.pallas_call(
        write_out,
        out_shape=(
            jax.ShapeDtypeStruct((2, DS), F32),
            jax.ShapeDtypeStruct((DS, COLS), BF16),
        ),
        in_specs=[pl.BlockSpec(memory_space=vm)] * 2,
        out_specs=(pl.BlockSpec(memory_space=pl.ANY), pl.BlockSpec(memory_space=pl.ANY)),
        scratch_shapes=[pltpu.SemaphoreType.DMA((1 + HCH,))],
        compiler_params=pltpu.CompilerParams(vmem_limit_bytes=1024 * 1024),
        name="write_out",
    )(sums, head)


def solution(mesh):
    placed = (P("grp", None), P("grp"), P(), P(None, ("grp", "vocab")), P("grp", None, "vocab"))
    return jax.shard_map(
        body,
        mesh=mesh,
        in_specs=placed,
        out_specs=(P(("grp", "vocab"), None), P(None, ("grp", "vocab"))),
        check_vma=False,
    )
```

```python
import functools

import jax
import jax.numpy as jnp
from jax import lax
from jax.experimental import pallas as pl
from jax.experimental.pallas import tpu as pltpu
from jax.sharding import PartitionSpec as P

MESH = pl.DeviceIdType.MESH
F32 = jnp.float32
BF16 = jnp.bfloat16
I32 = jnp.int32

DS = 3584
COLS = 512
GRPS = 4
ROWS = 512
GROWS = 128
NX, NY, NZ = 4, 4, 8

HROWS = GROWS // 2
HALF = ROWS // 2

YW = 640
ZW = 128
ZB = NY * YW

CW = DS // 2
SW = CW // 2

HCH = 7
HW = DS // HCH


def device(x, y, z, c):
    return (lax.div(x, 2) * 2 + c, (z * 2 + lax.rem(x, 2)) * 4 + y)


def merge(blocks):
    ms = functools.reduce(jnp.maximum, [b[0:1] for b in blocks])
    hard = soft = 0.0
    for b in blocks:
        d = jnp.exp((b[0:1] - ms) * 0.5)
        hard = hard + b[1:2] * (d * d)
        soft = soft + b[2:3] * d
    if blocks[0].shape[0] == 4:
        return ms, hard, soft
    mt = functools.reduce(jnp.maximum, [b[3:5] for b in blocks])
    teach = 0.0
    for b in blocks:
        teach = teach + jnp.exp(b[3:5] - mt)
    return ms, hard, soft, mt + jnp.log(teach)


def put(ref, stats):
    k = 0
    for s in stats:
        ref[k : k + s.shape[0], :] = s
        k += s.shape[0]


def kernel(
    hid, ids_hbm, srv_hbm, w_hbm, t_hbm, gh_out, ghead_out,
    ids, srv, h_all, w, wt, ht, tv, tst, tall, ids_all, pt, perm, lg, al, stc,
    sta, sta_x, sta_y, sta_z, stb, stb_x, stb_y, stb_z,
    fin, fint, rowf, rowt, g, gp, own, dsend, drecv, s1, r1, s1b, r1b, acc, s2, r2, acc3, s3f, s3, r3,
    ssem, rsem, lsem,
):
    gi = lax.axis_index("grp")
    vi = lax.axis_index("vocab")
    c = lax.rem(gi, 2)
    xh = lax.div(gi, 2)
    y = lax.rem(vi, 4)
    xl = lax.rem(lax.div(vi, 4), 2)
    z = lax.div(vi, 8)
    x = 2 * xh + xl
    other = device(x, y, z, 1 - c)
    partner = device(3 - x, y, z, c)
    xs = [device(lax.rem(x + k, NX), y, z, c) for k in range(1, NX)]
    ys = [device(x, lax.rem(y + k, NY), z, c) for k in range(1, NY)]
    zs = [device(x, y, lax.rem(z + k, NZ), c) for k in range(1, NZ)]
    xos = [device(lax.rem(x + k, NX), y, z, 1 - c) for k in range(1, NX)]

    bar = pltpu.get_barrier_semaphore()
    peers = [other, *xs, *xos, *ys, *zs]
    for p in peers:
        pl.semaphore_signal(bar, inc=1, device_id=p, device_id_type=MESH)

    count = [0]
    started = []

    def send(src, dst, to):
        k = count[0]
        count[0] += 1
        cp = pltpu.make_async_remote_copy(
            src_ref=src, dst_ref=dst, send_sem=ssem.at[k], recv_sem=rsem.at[k], device_id=to, device_id_type=MESH
        )
        cp.start()
        started.append(cp)
        return cp

    def load(src, dst, k):
        cp = pltpu.make_async_copy(src, dst, lsem.at[k])
        cp.start()
        return cp

    def await_all(cps):
        for cp in cps:
            cp.wait_recv()

    def rows_of(h):
        return pl.ds(h * HROWS, HROWS)

    load_ids = load(ids_hbm, ids, 0)
    load_srv = load(srv_hbm, srv, 1)
    load_t = load(t_hbm, tv, 2)
    load_h = [load(hid.at[rows_of(h)], h_all.at[h, gi], 3 + h) for h in range(2)]
    load_w = load(w_hbm, w, 5)

    load_ids.wait()
    load_srv.wait()
    pt[...] = (lax.broadcasted_iota(I32, (ROWS, ROWS), 0) == srv[...]).astype(BF16)
    ids_all[gi] = ids[...]
    for cp in load_h:
        cp.wait()

    pl.semaphore_wait(bar, len(peers))

    ycols = pl.ds(pl.multiple_of(y * YW, 128), YW)
    zcols = pl.ds(pl.multiple_of(ZB + z * ZW, ZW), ZW)
    cross_y, cross_z = [], []
    for h in range(2):
        for cols, cps in ((zcols, cross_z), (ycols, cross_y)):
            piece = h_all.at[h, gi, :, cols]
            cps.append(send(piece, piece, partner))
    pair = [send(h_all.at[h, gi], h_all.at[h, gi], other) for h in range(2)]
    idc = [send(ids_all.at[gi], ids_all.at[gi], (lax.rem(gi + k, GRPS), vi)) for k in range(1, GRPS)]

    load_t.wait()
    for q in range(GRPS):
        tst[q] = tv[:, q, :]
    t_all = tst[...].astype(F32)
    tm = jnp.max(jnp.max(t_all, axis=0), axis=1, keepdims=True)
    tsum = jnp.sum(jnp.sum(jnp.exp((t_all - tm[None]) * 0.5), axis=0), axis=1, keepdims=True)
    lse = jnp.broadcast_to(tm * 0.5 + jnp.log(tsum), (GROWS, 128)).T[0:1, :]
    none = jnp.full((1, GROWS), -1e30, F32)
    for j in range(GRPS):
        sta[0, 3 + j // 2 : 4 + j // 2, (j % 2) * GROWS : (j % 2 + 1) * GROWS] = jnp.where(gi == j, lse, none)

    gg = 2 * (1 - xh) + c
    fwd_y, fwd_z = [], []

    def forward(h):
        cross_z[h].wait_recv()
        piece = h_all.at[h, gg, :, zcols]
        fwd_z.append([send(piece, piece, p) for p in zs])
        cross_y[h].wait_recv()
        piece = h_all.at[h, gg, :, ycols]
        fwd_y.append([send(piece, piece, p) for p in ys])

    def share(h):
        cps = []
        for fwd, cols in ((fwd_y, pl.ds(0, ZB)), (fwd_z, pl.ds(ZB, NZ * ZW))):
            await_all(fwd[h])
            piece = h_all.at[h, gg, :, cols]
            cps.append(send(piece, piece, other))
        return cps

    def two_groups(part):
        return pl.ds(pl.multiple_of(part * GROWS, GROWS), GROWS)

    def logits(h, part):
        a = h_all[h, pl.ds(2 * part, 2)].reshape(GROWS, DS)
        lg[h, two_groups(part), :] = jnp.dot(a, w[...], preferred_element_type=F32)

    def student_stats(h, part):
        r = two_groups(part)
        l = lg[h, r, :]
        m = jnp.max(l, axis=1, keepdims=True)
        e = jnp.exp((l - m) * 0.5)
        lg[h, r, :] = e
        lane = lax.broadcasted_iota(I32, (GROWS, 128), 1)
        hard = jnp.sum(e * e, axis=1, keepdims=True)
        soft = jnp.sum(e, axis=1, keepdims=True)
        stc[h, r, :] = jnp.where(lane == 0, m, jnp.where(lane == 1, hard, soft))

    def turn_rows(h, part):
        cols = pl.ds(pl.multiple_of(h * HALF + part * GROWS, GROWS), GROWS)

        def step(i, _):
            s = pl.ds(pl.multiple_of(i * HW, HW), HW)
            ht[s, cols] = h_all[h, pl.ds(2 * part, 2), :, s].reshape(GROWS, HW).T
            return 0

        lax.fori_loop(0, HCH, step, 0)

    forward(0)
    load_w.wait()
    await_all(pair)
    logits(0, xh)
    forward(1)
    teach = []
    for k in range(1, GRPS):
        q = lax.rem(gi + k, GRPS)
        teach.append(send(tst.at[q], tall.at[gi], (q, vi)))
    tall[gi] = tst[gi]
    logits(1, xh)
    student_stats(0, xh)

    st = [sta, stb]
    st_x = [sta_x, stb_x]
    st_y = [sta_y, stb_y]
    st_z = [sta_z, stb_z]

    def stats_x(h):
        for j in range(2):
            s = slice(j * 128, (j + 1) * 128)
            st[h][0, 0:3, s] = stc[h, s, :].T[0:3, :]
        return [send(st[h].at[0], st_x[h].at[k], p) for k, p in enumerate([*xs, *xos, other])]

    def stats_y(h, cps):
        await_all(cps)
        put(st[h].at[2], merge([st[h][0], *[st_x[h][k] for k in range(2 * NX - 1)]]))
        return [send(st[h].at[2], st_y[h].at[k], p) for k, p in enumerate(ys)]

    def stats_z(h, cps):
        await_all(cps)
        put(st[h].at[3], merge([st[h][2], *[st_y[h][k] for k in range(NY - 1)]]))
        return [send(st[h].at[3], st_z[h].at[k], p) for k, p in enumerate(zs)]

    def stats_end(h, cps):
        await_all(cps)
        ms, hard, soft, *lse = merge([st[h][3], *[st_z[h][k] for k in range(NZ - 1)]])
        d = jnp.exp((st[h][0, 0:1, :] - ms) * 0.5)
        fin[0:1, :] = 32.0 * d / soft
        fin[1:2, :] = 16.0 * d * d / hard
        for j in range(2):
            s = slice(j * 128, (j + 1) * 128)
            fint[h, s, :] = fin[:, s].T
        return lse

    def turn_w(first, last):
        def step(i, _):
            s = pl.ds(pl.multiple_of(i * HW, HW), HW)
            wt[:, s] = w[s, :].T
            return 0

        lax.fori_loop(first, last, step, 0)

    def make_perm():
        i = lax.broadcasted_iota(I32, (HALF, 1), 0)
        i_c, hi, lo = lax.div(i, 128), lax.rem(lax.div(i, 32), 4), lax.rem(lax.div(i, 8), 4)
        i_z, i_b = lax.rem(lax.div(i, 2), 4), lax.rem(i, 2)
        col = lax.broadcasted_iota(I32, (HALF, HALF), 1)
        for p, (i_x, i_y) in enumerate(((hi, lo), (lo, hi))):
            r = (2 * lax.div(i_x, 2) + i_c) * HROWS + i_z * 16 + lax.rem(i_x, 2) * 8 + i_y * 2 + i_b
            perm[p] = (col == r).astype(BF16)

    fin[...] = jnp.zeros_like(fin)
    rowf[...] = jnp.zeros_like(rowf)
    shared = [share(0)]
    student_stats(1, xh)
    await_all(shared[0])
    logits(0, 1 - xh)
    student_stats(0, 1 - xh)
    m0 = stats_x(0)
    shared.append(share(1))
    await_all(shared[1])
    logits(1, 1 - xh)
    student_stats(1, 1 - xh)
    m1 = stats_x(1)
    m0 = stats_y(0, m0)
    make_perm()
    turn_w(0, 3)
    m0 = stats_z(0, m0)
    m1 = stats_y(1, m1)
    turn_w(3, HCH)

    await_all(teach)
    al[...] = lax.dot_general(
        pt[...], tall[...].reshape(ROWS, COLS), (((0,), (0,)), ((), ())), preferred_element_type=F32
    )
    await_all(idc)
    for j in range(GRPS):
        rowf[0:1, j * 128 : (j + 1) * 128] = ids_all[j].astype(F32)
    m1 = stats_z(1, m1)
    (lse,) = stats_end(0, m0)
    terms = 0.0
    for j in range(2):
        part = lse[j : j + 1, :]
        for k in range(3):
            term = part.astype(BF16).astype(F32)
            rowf[8 + k : 9 + k, j * HALF : (j + 1) * HALF] = term
            part = part - term
    terms = jnp.dot(rowf[8:16, :].astype(BF16), pt[...], preferred_element_type=F32)
    rowf[1:2, :] = terms[0:1] + terms[1:2] + terms[2:3]
    for j in range(4):
        s = slice(j * 128, (j + 1) * 128)
        rowt[s, :] = rowf[:, s].T

    first = (gi * (NX // 2 * NY * NZ) + vi) * COLS

    def grad(h):
        def step(j, _):
            r = pl.ds(pl.multiple_of(j * HROWS, HROWS), HROWS)
            full = pl.ds(pl.multiple_of(j * GROWS + h * HROWS, HROWS), HROWS)
            f = fint[h, r, :]
            f2 = rowt[full, :]
            e = lg[h, r, :]
            col = lax.broadcasted_iota(I32, (HROWS, COLS), 1) + first
            hit = jnp.where(f2[:, 0:1].astype(I32) == col, 16.0, 0.0)
            soft = e * f[:, 0:1] - 32.0 * jnp.exp(al[full, :] * 0.5 - f2[:, 1:2])
            g[pl.ds(pl.multiple_of(h * HALF + j * HROWS, HROWS), HROWS), :] = (
                soft + (e * e * f[:, 1:2] - hit)
            ).astype(BF16)
            return 0

        lax.fori_loop(0, GRPS, step, 0)
        for p in range(2):
            gp[p] = jnp.dot(perm[p], g[h * HALF : (h + 1) * HALF, :], preferred_element_type=F32).astype(BF16)

    pieces = [(p, i) for i in range(2) for p in range(2)]

    def partial(p, i, core):
        s = slice((2 * p + i) * SW, (2 * p + i + 1) * SW)
        return jnp.dot(gp[p, two_groups(core), :], wt[:, s], preferred_element_type=F32)

    def pair_stage(h):
        cps = {}
        for p, i in pieces:
            dsend[h, p, i] = partial(p, i, 1 - c).astype(BF16).reshape(4, 32, SW)
            cps[p, i] = send(dsend.at[h, p, i], drecv.at[h, p, i], other)
        return cps

    x_side = 2 * xh + 1 - xl
    y_side = y + 1 - 2 * lax.rem(y, 2)
    axes = [
        (x, ((3 - x, partner), (x_side, device(x_side, y, z, c))), y, ys),
        (y, ((3 - y, device(x, 3 - y, z, c)), (y_side, device(x, y_side, z, c))), x, xs),
    ]

    def chip_sum(h, p, i, k):
        return own[h, p, i, k] + drecv[h, p, i, k].astype(F32)

    def first_stage(h, cps):
        out = {}
        for p, i in pieces:
            own[h, p, i] = partial(p, i, c).reshape(4, 32, SW)
            cps[p, i].wait_recv()
            me, sides, _, _ = axes[p]
            place, to = sides[i]
            s1[h, p, i, 0] = chip_sum(h, p, i, place).astype(BF16)
            s1[h, p, i, 1] = chip_sum(h, p, i, lax.rem(me + 2, 4)).astype(BF16)
            out[p, i] = send(s1.at[h, p, i], r1.at[h, p, i], to)
        return out

    def first_stage_end(h, cps):
        out = {}
        for p, i in pieces:
            cps[p, i].wait_recv()
            place, to = axes[p][1][1 - i]
            s1b[h, p, i] = (chip_sum(h, p, i, place) + r1[h, p, i, 1].astype(F32)).astype(BF16)
            out[p, i] = send(s1b.at[h, p, i], r1b.at[h, p, i], to)
        return out

    def second_stage(h, cps):
        out = []
        for p in range(2):
            await_all([cps[p, 0], cps[p, 1]])
            me, _, me2, to = axes[p]
            t = [
                chip_sum(h, p, i, me) + (r1[h, p, i, 0].astype(F32) + r1b[h, p, i].astype(F32)) for i in range(2)
            ]
            for j in range(4):
                r = slice(j * 8, (j + 1) * 8)
                acc[h, p, j, :, :SW] = t[0][r]
                acc[h, p, j, :, SW:] = t[1][r]
                s2[h, p, j] = jnp.concatenate([t[0][r], t[1][r]], axis=0).astype(BF16)
            out.append([send(s2.at[h, p, lax.rem(me2 + k, 4)], r2.at[h, p, k - 1], d) for k, d in enumerate(to, 1)])
        return out

    base3 = 120
    s3f[:, 14:16, :] = jnp.zeros((NZ, 2, 512), F32)

    def third_copy(k, to):
        return pltpu.make_async_remote_copy(
            src_ref=s3.at[to],
            dst_ref=r3.at[k - 1],
            send_sem=ssem.at[base3 + k],
            recv_sem=rsem.at[base3 + k],
            device_id=device(x, y, to, c),
            device_id_type=MESH,
        )

    def third_stage(h, parts):
        for p, cps in enumerate(parts):
            await_all(cps)
            t = acc[h, p, axes[p][2]]
            u = r2[h, p, 0].astype(F32) + r2[h, p, 1].astype(F32) + r2[h, p, 2].astype(F32)
            base = p * CW
            acc3[:, base : base + SW] = t[:, : SW] + u[0:8]
            acc3[:, base + SW : base + CW] = t[:, SW :] + u[8:16]
        for j in range(4):
            for k in range(DS // 512):
                s3f[4 * h + j, 2 * k : 2 * k + 2, :] = acc3[2 * j : 2 * j + 2, k * 512 : (k + 1) * 512]
            s3[4 * h + j] = s3f[4 * h + j].astype(BF16)
        for k in range(1, NZ):
            to = lax.rem(z + k, NZ)

            @pl.when(lax.div(to, 4) == h)
            def _():
                third_copy(k, to).start()

    def third_end():
        for k in range(1, NZ):
            third_copy(k, lax.rem(z + k, NZ)).wait_recv()
        t = s3f[z]
        for k in range(NZ - 1):
            t = t + r3[k].astype(F32)
        for k in range(DS // 512):
            gh_out[:, k * 512 : (k + 1) * 512] = t[2 * k : 2 * k + 2, :]
        for k in range(1, NZ):
            third_copy(k, lax.rem(z + k, NZ)).wait_send()

    def head(first, last):
        def step(k, _):
            s = pl.ds(pl.multiple_of(k * HW, HW), HW)
            ghead_out[s, :] = jnp.dot(ht[s, :], g[...], preferred_element_type=F32).astype(BF16)
            return 0

        lax.fori_loop(first, last, step, 0)

    grad(0)
    m0 = pair_stage(0)
    m0 = first_stage(0, m0)
    stats_end(1, m1)
    grad(1)
    m1 = pair_stage(1)
    m0 = first_stage_end(0, m0)
    m1 = first_stage(1, m1)
    for h in range(2):
        turn_rows(h, xh)
    m0 = second_stage(0, m0)
    m1 = first_stage_end(1, m1)
    for h in range(2):
        turn_rows(h, 1 - xh)
    head(0, 2)
    third_stage(0, m0)
    m1 = second_stage(1, m1)
    head(2, HCH)
    third_stage(1, m1)
    third_end()

    for cp in started:
        cp.wait_send()


def write_out(sums, head, gh_out, ghead_out, sem):
    cps = [pltpu.make_async_copy(sums, gh_out, sem.at[HCH])]
    for k in range(HCH):
        s = pl.ds(k * HW, HW)
        cps.append(pltpu.make_async_copy(head.at[s], ghead_out.at[s], sem.at[k]))
    for cp in cps:
        cp.start()
    for cp in cps:
        cp.wait()


N_SEMS = 128


def body(hidden, token_ids, serving, head_weight, teacher_logits):
    vm = pltpu.VMEM
    sums, head = pl.pallas_call(
        kernel,
        out_shape=(
            vm((2, DS), F32),
            vm((DS, COLS), BF16),
        ),
        in_specs=[pl.BlockSpec(memory_space=pltpu.HBM)] * 5,
        out_specs=(pl.BlockSpec(memory_space=vm), pl.BlockSpec(memory_space=vm)),
        scratch_shapes=[
            vm((1, GROWS), I32),
            vm((1, ROWS), I32),
            vm((2, GRPS, HROWS, DS), BF16),
            vm((DS, COLS), BF16),
            vm((COLS, DS), BF16),
            vm((DS, ROWS), BF16),
            vm((GROWS, GRPS, COLS), BF16),
            vm((GRPS, GROWS, COLS), BF16),
            vm((GRPS, GROWS, COLS), BF16),
            vm((GRPS, 1, GROWS), I32),
            vm((ROWS, ROWS), BF16),
            vm((2, HALF, HALF), BF16),
            vm((2, HALF, COLS), F32),
            vm((ROWS, COLS), F32),
            vm((2, HALF, 128), F32),
            vm((4, 8, HALF), F32),
            vm((2 * NX - 1, 8, HALF), F32),
            vm((NY - 1, 8, HALF), F32),
            vm((NZ - 1, 8, HALF), F32),
            vm((4, 4, HALF), F32),
            vm((2 * NX - 1, 4, HALF), F32),
            vm((NY - 1, 4, HALF), F32),
            vm((NZ - 1, 4, HALF), F32),
            vm((128, HALF), F32),
            vm((2, HALF, 128), F32),
            vm((128, ROWS), F32),
            vm((ROWS, 128), F32),
            vm((ROWS, COLS), BF16),
            vm((2, HALF, COLS), BF16),
            vm((2, 2, 2, 4, 32, SW), F32),
            vm((2, 2, 2, 4, 32, SW), BF16),
            vm((2, 2, 2, 4, 32, SW), BF16),
            vm((2, 2, 2, 2, 32, SW), BF16),
            vm((2, 2, 2, 2, 32, SW), BF16),
            vm((2, 2, 2, 32, SW), BF16),
            vm((2, 2, 2, 32, SW), BF16),
            vm((2, 2, 4, 8, CW), F32),
            vm((2, 2, 4, 16, SW), BF16),
            vm((2, 2, 3, 16, SW), BF16),
            vm((8, DS), F32),
            vm((NZ, 16, 512), F32),
            vm((NZ, 16, 512), BF16),
            vm((NZ - 1, 16, 512), BF16),
            pltpu.SemaphoreType.DMA((N_SEMS,)),
            pltpu.SemaphoreType.DMA((N_SEMS,)),
            pltpu.SemaphoreType.DMA((6,)),
        ],
        compiler_params=pltpu.CompilerParams(
            collective_id=0, has_side_effects=True, vmem_limit_bytes=48 * 1024 * 1024
        ),
        name="distill_backward",
    )(*[
        pltpu.with_memory_space_constraint(a, pltpu.HBM)
        for a in (hidden, token_ids.reshape(1, GROWS), serving.reshape(1, ROWS), head_weight, teacher_logits)
    ])
    return pl.pallas_call(
        write_out,
        out_shape=(
            jax.ShapeDtypeStruct((2, DS), F32),
            jax.ShapeDtypeStruct((DS, COLS), BF16),
        ),
        in_specs=[pl.BlockSpec(memory_space=vm)] * 2,
        out_specs=(pl.BlockSpec(memory_space=pl.ANY), pl.BlockSpec(memory_space=pl.ANY)),
        scratch_shapes=[pltpu.SemaphoreType.DMA((1 + HCH,))],
        compiler_params=pltpu.CompilerParams(vmem_limit_bytes=1024 * 1024),
        name="write_out",
    )(sums, head)


def solution(mesh):
    placed = (P("grp", None), P("grp"), P(), P(None, ("grp", "vocab")), P("grp", None, "vocab"))
    return jax.shard_map(
        body,
        mesh=mesh,
        in_specs=placed,
        out_specs=(P(("grp", "vocab"), None), P(None, ("grp", "vocab"))),
        check_vma=False,
    )
```

```python
import functools

import jax
import jax.numpy as jnp
from jax import lax
from jax.experimental import pallas as pl
from jax.experimental.pallas import tpu as pltpu
from jax.sharding import PartitionSpec as P

MESH = pl.DeviceIdType.MESH
F32 = jnp.float32
BF16 = jnp.bfloat16
I32 = jnp.int32

DS = 3584
COLS = 512
GRPS = 4
ROWS = 512
GROWS = 128
NX, NY, NZ = 4, 4, 8

HROWS = GROWS // 2
HALF = ROWS // 2

YW = 640
ZW = 128
ZB = NY * YW

CW = DS // 2
SW = CW // 2

HCH = 7
HW = DS // HCH


def device(x, y, z, c):
    return (lax.div(x, 2) * 2 + c, (z * 2 + lax.rem(x, 2)) * 4 + y)


def merge(blocks):
    ms = functools.reduce(jnp.maximum, [b[0:1] for b in blocks])
    hard = soft = 0.0
    for b in blocks:
        d = jnp.exp((b[0:1] - ms) * 0.5)
        hard = hard + b[1:2] * (d * d)
        soft = soft + b[2:3] * d
    if blocks[0].shape[0] == 4:
        return ms, hard, soft
    mt = functools.reduce(jnp.maximum, [b[3:5] for b in blocks])
    teach = 0.0
    for b in blocks:
        teach = teach + jnp.exp(b[3:5] - mt)
    return ms, hard, soft, mt + jnp.log(teach)


def put(ref, stats):
    k = 0
    for s in stats:
        ref[k : k + s.shape[0], :] = s
        k += s.shape[0]


def kernel(
    hid, ids_hbm, srv_hbm, w_hbm, t_hbm, gh_out, ghead_out,
    ids, srv, h_all, w, wt, ht, tv, tst, tall, ids_all, pt, perm, lg, al, stc,
    sta, sta_x, sta_y, sta_z, stb, stb_x, stb_y, stb_z,
    fin, fint, rowf, rowt, g, gp, own, dsend, drecv, s1, r1, s1b, r1b, acc, s2, r2, acc3, s3f, s3, r3,
    ssem, rsem, lsem,
):
    gi = lax.axis_index("grp")
    vi = lax.axis_index("vocab")
    c = lax.rem(gi, 2)
    xh = lax.div(gi, 2)
    y = lax.rem(vi, 4)
    xl = lax.rem(lax.div(vi, 4), 2)
    z = lax.div(vi, 8)
    x = 2 * xh + xl
    other = device(x, y, z, 1 - c)
    partner = device(3 - x, y, z, c)
    xs = [device(lax.rem(x + k, NX), y, z, c) for k in range(1, NX)]
    ys = [device(x, lax.rem(y + k, NY), z, c) for k in range(1, NY)]
    zs = [device(x, y, lax.rem(z + k, NZ), c) for k in range(1, NZ)]
    xos = [device(lax.rem(x + k, NX), y, z, 1 - c) for k in range(1, NX)]

    bar = pltpu.get_barrier_semaphore()
    peers = [other, *xs, *xos, *ys, *zs]
    for p in peers:
        pl.semaphore_signal(bar, inc=1, device_id=p, device_id_type=MESH)

    count = [0]
    started = []

    def send(src, dst, to):
        k = count[0]
        count[0] += 1
        cp = pltpu.make_async_remote_copy(
            src_ref=src, dst_ref=dst, send_sem=ssem.at[k], recv_sem=rsem.at[k], device_id=to, device_id_type=MESH
        )
        cp.start()
        started.append(cp)
        return cp

    def load(src, dst, k):
        cp = pltpu.make_async_copy(src, dst, lsem.at[k])
        cp.start()
        return cp

    def await_all(cps):
        for cp in cps:
            cp.wait_recv()

    def rows_of(h):
        return pl.ds(h * HROWS, HROWS)

    load_ids = load(ids_hbm, ids, 0)
    load_srv = load(srv_hbm, srv, 1)
    load_t = load(t_hbm, tv, 2)
    load_h = [load(hid.at[rows_of(h)], h_all.at[h, gi], 3 + h) for h in range(2)]
    load_w = load(w_hbm, w, 5)

    load_ids.wait()
    load_srv.wait()
    pt[...] = (lax.broadcasted_iota(I32, (ROWS, ROWS), 0) == srv[...]).astype(BF16)
    ids_all[gi] = ids[...]
    for cp in load_h:
        cp.wait()

    pl.semaphore_wait(bar, len(peers))

    ycols = pl.ds(pl.multiple_of(y * YW, 128), YW)
    zcols = pl.ds(pl.multiple_of(ZB + z * ZW, ZW), ZW)
    cross_y, cross_z = [], []
    for h in range(2):
        for cols, cps in ((zcols, cross_z), (ycols, cross_y)):
            piece = h_all.at[h, gi, :, cols]
            cps.append(send(piece, piece, partner))
    pair = [send(h_all.at[h, gi], h_all.at[h, gi], other) for h in range(2)]
    idc = [send(ids_all.at[gi], ids_all.at[gi], (lax.rem(gi + k, GRPS), vi)) for k in range(1, GRPS)]

    gg = 2 * (1 - xh) + c
    fwd_y, fwd_z = [], []

    def forward(h):
        cross_z[h].wait_recv()
        piece = h_all.at[h, gg, :, zcols]
        fwd_z.append([send(piece, piece, p) for p in zs])
        cross_y[h].wait_recv()
        piece = h_all.at[h, gg, :, ycols]
        fwd_y.append([send(piece, piece, p) for p in ys])

    def share(h):
        cps = []
        for fwd, cols in ((fwd_y, pl.ds(0, ZB)), (fwd_z, pl.ds(ZB, NZ * ZW))):
            await_all(fwd[h])
            piece = h_all.at[h, gg, :, cols]
            cps.append(send(piece, piece, other))
        return cps

    def two_groups(part):
        return pl.ds(pl.multiple_of(part * GROWS, GROWS), GROWS)

    def logits(h, part):
        a = h_all[h, pl.ds(2 * part, 2)].reshape(GROWS, DS)
        lg[h, two_groups(part), :] = jnp.dot(a, w[...], preferred_element_type=F32)

    def student_stats(h, part):
        r = two_groups(part)
        l = lg[h, r, :]
        m = jnp.max(l, axis=1, keepdims=True)
        e = jnp.exp((l - m) * 0.5)
        lg[h, r, :] = e
        lane = lax.broadcasted_iota(I32, (GROWS, 128), 1)
        hard = jnp.sum(e * e, axis=1, keepdims=True)
        soft = jnp.sum(e, axis=1, keepdims=True)
        stc[h, r, :] = jnp.where(lane == 0, m, jnp.where(lane == 1, hard, soft))

    def turn_rows(h, part):
        cols = pl.ds(pl.multiple_of(h * HALF + part * GROWS, GROWS), GROWS)

        def step(i, _):
            s = pl.ds(pl.multiple_of(i * HW, HW), HW)
            ht[s, cols] = h_all[h, pl.ds(2 * part, 2), :, s].reshape(GROWS, HW).T
            return 0

        lax.fori_loop(0, HCH, step, 0)

    forward(0)
    load_w.wait()
    await_all(pair)
    logits(0, xh)
    load_t.wait()
    for q in range(GRPS):
        tst[q] = tv[:, q, :]
    t_all = tst[...].astype(F32)
    tm = jnp.max(jnp.max(t_all, axis=0), axis=1, keepdims=True)
    tsum = jnp.sum(jnp.sum(jnp.exp((t_all - tm[None]) * 0.5), axis=0), axis=1, keepdims=True)
    lse = jnp.broadcast_to(tm * 0.5 + jnp.log(tsum), (GROWS, 128)).T[0:1, :]
    none = jnp.full((1, GROWS), -1e30, F32)
    for j in range(GRPS):
        sta[0, 3 + j // 2 : 4 + j // 2, (j % 2) * GROWS : (j % 2 + 1) * GROWS] = jnp.where(gi == j, lse, none)
    forward(1)
    teach = []
    for k in range(1, GRPS):
        q = lax.rem(gi + k, GRPS)
        teach.append(send(tst.at[q], tall.at[gi], (q, vi)))
    tall[gi] = tst[gi]
    logits(1, xh)
    student_stats(0, xh)

    st = [sta, stb]
    st_x = [sta_x, stb_x]
    st_y = [sta_y, stb_y]
    st_z = [sta_z, stb_z]

    def stats_x(h):
        for j in range(2):
            s = slice(j * 128, (j + 1) * 128)
            st[h][0, 0:3, s] = stc[h, s, :].T[0:3, :]
        return [send(st[h].at[0], st_x[h].at[k], p) for k, p in enumerate([*xs, *xos, other])]

    def stats_y(h, cps):
        await_all(cps)
        put(st[h].at[2], merge([st[h][0], *[st_x[h][k] for k in range(2 * NX - 1)]]))
        return [send(st[h].at[2], st_y[h].at[k], p) for k, p in enumerate(ys)]

    def stats_z(h, cps):
        await_all(cps)
        put(st[h].at[3], merge([st[h][2], *[st_y[h][k] for k in range(NY - 1)]]))
        return [send(st[h].at[3], st_z[h].at[k], p) for k, p in enumerate(zs)]

    def stats_end(h, cps):
        await_all(cps)
        ms, hard, soft, *lse = merge([st[h][3], *[st_z[h][k] for k in range(NZ - 1)]])
        d = jnp.exp((st[h][0, 0:1, :] - ms) * 0.5)
        fin[0:1, :] = 32.0 * d / soft
        fin[1:2, :] = 16.0 * d * d / hard
        for j in range(2):
            s = slice(j * 128, (j + 1) * 128)
            fint[h, s, :] = fin[:, s].T
        return lse

    def turn_w(first, last):
        def step(i, _):
            s = pl.ds(pl.multiple_of(i * HW, HW), HW)
            wt[:, s] = w[s, :].T
            return 0

        lax.fori_loop(first, last, step, 0)

    def make_perm():
        i = lax.broadcasted_iota(I32, (HALF, 1), 0)
        i_c, hi, lo = lax.div(i, 128), lax.rem(lax.div(i, 32), 4), lax.rem(lax.div(i, 8), 4)
        i_z, i_b = lax.rem(lax.div(i, 2), 4), lax.rem(i, 2)
        col = lax.broadcasted_iota(I32, (HALF, HALF), 1)
        for p, (i_x, i_y) in enumerate(((hi, lo), (lo, hi))):
            r = (2 * lax.div(i_x, 2) + i_c) * HROWS + i_z * 16 + lax.rem(i_x, 2) * 8 + i_y * 2 + i_b
            perm[p] = (col == r).astype(BF16)

    fin[...] = jnp.zeros_like(fin)
    rowf[...] = jnp.zeros_like(rowf)
    shared = [share(0)]
    student_stats(1, xh)
    await_all(shared[0])
    logits(0, 1 - xh)
    student_stats(0, 1 - xh)
    m0 = stats_x(0)
    shared.append(share(1))
    await_all(shared[1])
    logits(1, 1 - xh)
    student_stats(1, 1 - xh)
    m1 = stats_x(1)
    m0 = stats_y(0, m0)
    make_perm()
    turn_w(0, 3)
    m0 = stats_z(0, m0)
    m1 = stats_y(1, m1)
    turn_w(3, HCH)

    await_all(teach)
    al[...] = lax.dot_general(
        pt[...], tall[...].reshape(ROWS, COLS), (((0,), (0,)), ((), ())), preferred_element_type=F32
    )
    await_all(idc)
    for j in range(GRPS):
        rowf[0:1, j * 128 : (j + 1) * 128] = ids_all[j].astype(F32)
    m1 = stats_z(1, m1)
    (lse,) = stats_end(0, m0)
    terms = 0.0
    for j in range(2):
        part = lse[j : j + 1, :]
        for k in range(3):
            term = part.astype(BF16).astype(F32)
            rowf[8 + k : 9 + k, j * HALF : (j + 1) * HALF] = term
            part = part - term
    terms = jnp.dot(rowf[8:16, :].astype(BF16), pt[...], preferred_element_type=F32)
    rowf[1:2, :] = terms[0:1] + terms[1:2] + terms[2:3]
    for j in range(4):
        s = slice(j * 128, (j + 1) * 128)
        rowt[s, :] = rowf[:, s].T

    first = (gi * (NX // 2 * NY * NZ) + vi) * COLS

    def teacher_part(h):
        def step(j, _):
            full = pl.ds(pl.multiple_of(j * GROWS + h * HROWS, HROWS), HROWS)
            f = rowt[full, :]
            col = lax.broadcasted_iota(I32, (HROWS, COLS), 1) + first
            hit = jnp.where(f[:, 0:1].astype(I32) == col, 16.0, 0.0)
            al[full, :] = 32.0 * jnp.exp(al[full, :] * 0.5 - f[:, 1:2]) + hit
            return 0

        lax.fori_loop(0, GRPS, step, 0)

    def grad(h):
        def step(j, _):
            r = pl.ds(pl.multiple_of(j * HROWS, HROWS), HROWS)
            full = pl.ds(pl.multiple_of(j * GROWS + h * HROWS, HROWS), HROWS)
            f = fint[h, r, :]
            e = lg[h, r, :]
            g[pl.ds(pl.multiple_of(h * HALF + j * HROWS, HROWS), HROWS), :] = (
                e * (f[:, 0:1] + e * f[:, 1:2]) - al[full, :]
            ).astype(BF16)
            return 0

        lax.fori_loop(0, GRPS, step, 0)
        for p in range(2):
            gp[p] = jnp.dot(perm[p], g[h * HALF : (h + 1) * HALF, :], preferred_element_type=F32).astype(BF16)

    pieces = [(p, i) for i in range(2) for p in range(2)]

    def partial(p, i, core):
        s = slice((2 * p + i) * SW, (2 * p + i + 1) * SW)
        return jnp.dot(gp[p, two_groups(core), :], wt[:, s], preferred_element_type=F32)

    def pair_stage(h):
        cps = {}
        for p, i in pieces:
            dsend[h, p, i] = partial(p, i, 1 - c).astype(BF16).reshape(4, 32, SW)
            cps[p, i] = send(dsend.at[h, p, i], drecv.at[h, p, i], other)
        return cps

    x_side = 2 * xh + 1 - xl
    y_side = y + 1 - 2 * lax.rem(y, 2)
    axes = [
        (x, ((3 - x, partner), (x_side, device(x_side, y, z, c))), y, ys),
        (y, ((3 - y, device(x, 3 - y, z, c)), (y_side, device(x, y_side, z, c))), x, xs),
    ]

    def chip_sum(h, p, i, k):
        return own[h, p, i, k] + drecv[h, p, i, k].astype(F32)

    def first_stage(h, cps):
        out = {}
        for p, i in pieces:
            own[h, p, i] = partial(p, i, c).reshape(4, 32, SW)
            cps[p, i].wait_recv()
            me, sides, _, _ = axes[p]
            place, to = sides[i]
            s1[h, p, i, 0] = chip_sum(h, p, i, place).astype(BF16)
            s1[h, p, i, 1] = chip_sum(h, p, i, lax.rem(me + 2, 4)).astype(BF16)
            out[p, i] = send(s1.at[h, p, i], r1.at[h, p, i], to)
        return out

    def first_stage_end(h, cps):
        out = {}
        for p, i in pieces:
            cps[p, i].wait_recv()
            place, to = axes[p][1][1 - i]
            s1b[h, p, i] = (chip_sum(h, p, i, place) + r1[h, p, i, 1].astype(F32)).astype(BF16)
            out[p, i] = send(s1b.at[h, p, i], r1b.at[h, p, i], to)
        return out

    def second_stage(h, cps):
        out = []
        for p in range(2):
            await_all([cps[p, 0], cps[p, 1]])
            me, _, me2, to = axes[p]
            t = [
                chip_sum(h, p, i, me) + (r1[h, p, i, 0].astype(F32) + r1b[h, p, i].astype(F32)) for i in range(2)
            ]
            for j in range(4):
                r = slice(j * 8, (j + 1) * 8)
                acc[h, p, j, :, :SW] = t[0][r]
                acc[h, p, j, :, SW:] = t[1][r]
                s2[h, p, j] = jnp.concatenate([t[0][r], t[1][r]], axis=0).astype(BF16)
            out.append([send(s2.at[h, p, lax.rem(me2 + k, 4)], r2.at[h, p, k - 1], d) for k, d in enumerate(to, 1)])
        return out

    base3 = 120
    s3f[:, 14:16, :] = jnp.zeros((NZ, 2, 512), F32)

    def third_copy(k, to):
        return pltpu.make_async_remote_copy(
            src_ref=s3.at[to],
            dst_ref=r3.at[k - 1],
            send_sem=ssem.at[base3 + k],
            recv_sem=rsem.at[base3 + k],
            device_id=device(x, y, to, c),
            device_id_type=MESH,
        )

    def third_stage(h, parts):
        for p, cps in enumerate(parts):
            await_all(cps)
            t = acc[h, p, axes[p][2]]
            u = r2[h, p, 0].astype(F32) + r2[h, p, 1].astype(F32) + r2[h, p, 2].astype(F32)
            base = p * CW
            acc3[:, base : base + SW] = t[:, : SW] + u[0:8]
            acc3[:, base + SW : base + CW] = t[:, SW :] + u[8:16]
        for j in range(4):
            for k in range(DS // 512):
                s3f[4 * h + j, 2 * k : 2 * k + 2, :] = acc3[2 * j : 2 * j + 2, k * 512 : (k + 1) * 512]
            s3[4 * h + j] = s3f[4 * h + j].astype(BF16)
        for k in range(1, NZ):
            to = lax.rem(z + k, NZ)

            @pl.when(lax.div(to, 4) == h)
            def _():
                third_copy(k, to).start()

    def third_end():
        for k in range(1, NZ):
            third_copy(k, lax.rem(z + k, NZ)).wait_recv()
        t = s3f[z]
        for k in range(NZ - 1):
            t = t + r3[k].astype(F32)
        for k in range(DS // 512):
            gh_out[:, k * 512 : (k + 1) * 512] = t[2 * k : 2 * k + 2, :]
        for k in range(1, NZ):
            third_copy(k, lax.rem(z + k, NZ)).wait_send()

    def head(first, last):
        def step(k, _):
            s = pl.ds(pl.multiple_of(k * HW, HW), HW)
            ghead_out[s, :] = jnp.dot(ht[s, :], g[...], preferred_element_type=F32).astype(BF16)
            return 0

        lax.fori_loop(first, last, step, 0)

    teacher_part(0)
    grad(0)
    m0 = pair_stage(0)
    teacher_part(1)
    m0 = first_stage(0, m0)
    stats_end(1, m1)
    grad(1)
    m1 = pair_stage(1)
    m1 = first_stage(1, m1)
    m0 = first_stage_end(0, m0)
    for h in range(2):
        turn_rows(h, xh)
    m0 = second_stage(0, m0)
    m1 = first_stage_end(1, m1)
    for h in range(2):
        turn_rows(h, 1 - xh)
    head(0, 2)
    third_stage(0, m0)
    m1 = second_stage(1, m1)
    head(2, HCH)
    third_stage(1, m1)
    third_end()

    for cp in started:
        cp.wait_send()


def write_out(sums, head, gh_out, ghead_out, sem):
    cps = [pltpu.make_async_copy(sums, gh_out, sem.at[HCH])]
    for k in range(HCH):
        s = pl.ds(k * HW, HW)
        cps.append(pltpu.make_async_copy(head.at[s], ghead_out.at[s], sem.at[k]))
    for cp in cps:
        cp.start()
    for cp in cps:
        cp.wait()


N_SEMS = 128


def body(hidden, token_ids, serving, head_weight, teacher_logits):
    vm = pltpu.VMEM
    sums, head = pl.pallas_call(
        kernel,
        out_shape=(
            vm((2, DS), F32),
            vm((DS, COLS), BF16),
        ),
        in_specs=[pl.BlockSpec(memory_space=pltpu.HBM)] * 5,
        out_specs=(pl.BlockSpec(memory_space=vm), pl.BlockSpec(memory_space=vm)),
        scratch_shapes=[
            vm((1, GROWS), I32),
            vm((1, ROWS), I32),
            vm((2, GRPS, HROWS, DS), BF16),
            vm((DS, COLS), BF16),
            vm((COLS, DS), BF16),
            vm((DS, ROWS), BF16),
            vm((GROWS, GRPS, COLS), BF16),
            vm((GRPS, GROWS, COLS), BF16),
            vm((GRPS, GROWS, COLS), BF16),
            vm((GRPS, 1, GROWS), I32),
            vm((ROWS, ROWS), BF16),
            vm((2, HALF, HALF), BF16),
            vm((2, HALF, COLS), F32),
            vm((ROWS, COLS), F32),
            vm((2, HALF, 128), F32),
            vm((4, 8, HALF), F32),
            vm((2 * NX - 1, 8, HALF), F32),
            vm((NY - 1, 8, HALF), F32),
            vm((NZ - 1, 8, HALF), F32),
            vm((4, 4, HALF), F32),
            vm((2 * NX - 1, 4, HALF), F32),
            vm((NY - 1, 4, HALF), F32),
            vm((NZ - 1, 4, HALF), F32),
            vm((128, HALF), F32),
            vm((2, HALF, 128), F32),
            vm((128, ROWS), F32),
            vm((ROWS, 128), F32),
            vm((ROWS, COLS), BF16),
            vm((2, HALF, COLS), BF16),
            vm((2, 2, 2, 4, 32, SW), F32),
            vm((2, 2, 2, 4, 32, SW), BF16),
            vm((2, 2, 2, 4, 32, SW), BF16),
            vm((2, 2, 2, 2, 32, SW), BF16),
            vm((2, 2, 2, 2, 32, SW), BF16),
            vm((2, 2, 2, 32, SW), BF16),
            vm((2, 2, 2, 32, SW), BF16),
            vm((2, 2, 4, 8, CW), F32),
            vm((2, 2, 4, 16, SW), BF16),
            vm((2, 2, 3, 16, SW), BF16),
            vm((8, DS), F32),
            vm((NZ, 16, 512), F32),
            vm((NZ, 16, 512), BF16),
            vm((NZ - 1, 16, 512), BF16),
            pltpu.SemaphoreType.DMA((N_SEMS,)),
            pltpu.SemaphoreType.DMA((N_SEMS,)),
            pltpu.SemaphoreType.DMA((6,)),
        ],
        compiler_params=pltpu.CompilerParams(
            collective_id=0, has_side_effects=True, vmem_limit_bytes=48 * 1024 * 1024
        ),
        name="distill_backward",
    )(*[
        pltpu.with_memory_space_constraint(a, pltpu.HBM)
        for a in (hidden, token_ids.reshape(1, GROWS), serving.reshape(1, ROWS), head_weight, teacher_logits)
    ])
    return pl.pallas_call(
        write_out,
        out_shape=(
            jax.ShapeDtypeStruct((2, DS), F32),
            jax.ShapeDtypeStruct((DS, COLS), BF16),
        ),
        in_specs=[pl.BlockSpec(memory_space=vm)] * 2,
        out_specs=(pl.BlockSpec(memory_space=pl.ANY), pl.BlockSpec(memory_space=pl.ANY)),
        scratch_shapes=[pltpu.SemaphoreType.DMA((1 + HCH,))],
        compiler_params=pltpu.CompilerParams(vmem_limit_bytes=1024 * 1024),
        name="write_out",
    )(sums, head)


def solution(mesh):
    placed = (P("grp", None), P("grp"), P(), P(None, ("grp", "vocab")), P("grp", None, "vocab"))
    return jax.shard_map(
        body,
        mesh=mesh,
        in_specs=placed,
        out_specs=(P(("grp", "vocab"), None), P(None, ("grp", "vocab"))),
        check_vma=False,
    )
```

```python
import functools

import jax
import jax.numpy as jnp
from jax import lax
from jax.experimental import pallas as pl
from jax.experimental.pallas import tpu as pltpu
from jax.sharding import PartitionSpec as P

MESH = pl.DeviceIdType.MESH
F32 = jnp.float32
BF16 = jnp.bfloat16
I32 = jnp.int32

DS = 3584
COLS = 512
GRPS = 4
ROWS = 512
GROWS = 128
NX, NY, NZ = 4, 4, 8

HROWS = GROWS // 2
HALF = ROWS // 2

YW = 640
ZW = 128
ZB = NY * YW

CW = DS // 2
SW = CW // 2

HCH = 7
HW = DS // HCH


def device(x, y, z, c):
    return (lax.div(x, 2) * 2 + c, (z * 2 + lax.rem(x, 2)) * 4 + y)


def merge(blocks):
    ms = functools.reduce(jnp.maximum, [b[0:1] for b in blocks])
    hard = soft = 0.0
    for b in blocks:
        d = jnp.exp((b[0:1] - ms) * 0.5)
        hard = hard + b[1:2] * (d * d)
        soft = soft + b[2:3] * d
    if blocks[0].shape[0] == 4:
        return ms, hard, soft
    mt = functools.reduce(jnp.maximum, [b[3:5] for b in blocks])
    teach = 0.0
    for b in blocks:
        teach = teach + jnp.exp(b[3:5] - mt)
    return ms, hard, soft, mt + jnp.log(teach)


def put(ref, stats):
    k = 0
    for s in stats:
        ref[k : k + s.shape[0], :] = s
        k += s.shape[0]


def kernel(
    hid, ids_hbm, srv_hbm, w_hbm, t_hbm, gh_out, ghead_out,
    ids, srv, h_all, w, wt, ht, tv, tst, tall, ids_all, pt, perm, lg, al, stc,
    sta, sta_x, sta_y, sta_z, stb, stb_x, stb_y, stb_z,
    fin, fint, rowf, rowt, g, gp, own, dsend, drecv, s1, r1, s1b, r1b, acc, s2, r2, acc3, s3f, s3, r3,
    ssem, rsem, lsem,
):
    gi = lax.axis_index("grp")
    vi = lax.axis_index("vocab")
    c = lax.rem(gi, 2)
    xh = lax.div(gi, 2)
    y = lax.rem(vi, 4)
    xl = lax.rem(lax.div(vi, 4), 2)
    z = lax.div(vi, 8)
    x = 2 * xh + xl
    other = device(x, y, z, 1 - c)
    partner = device(3 - x, y, z, c)
    xs = [device(lax.rem(x + k, NX), y, z, c) for k in range(1, NX)]
    ys = [device(x, lax.rem(y + k, NY), z, c) for k in range(1, NY)]
    zs = [device(x, y, lax.rem(z + k, NZ), c) for k in range(1, NZ)]
    xos = [device(lax.rem(x + k, NX), y, z, 1 - c) for k in range(1, NX)]

    bar = pltpu.get_barrier_semaphore()
    peers = [other, *xs, *xos, *ys, *zs]
    for p in peers:
        pl.semaphore_signal(bar, inc=1, device_id=p, device_id_type=MESH)

    count = [0]
    started = []

    def send(src, dst, to):
        k = count[0]
        count[0] += 1
        cp = pltpu.make_async_remote_copy(
            src_ref=src, dst_ref=dst, send_sem=ssem.at[k], recv_sem=rsem.at[k], device_id=to, device_id_type=MESH
        )
        cp.start()
        started.append(cp)
        return cp

    def load(src, dst, k):
        cp = pltpu.make_async_copy(src, dst, lsem.at[k])
        cp.start()
        return cp

    def await_all(cps):
        for cp in cps:
            cp.wait_recv()

    def rows_of(h):
        return pl.ds(h * HROWS, HROWS)

    load_ids = load(ids_hbm, ids, 0)
    load_srv = load(srv_hbm, srv, 1)
    load_t = load(t_hbm, tv, 2)
    load_h = [load(hid.at[rows_of(h)], h_all.at[h, gi], 3 + h) for h in range(2)]
    load_w = load(w_hbm, w, 5)

    load_ids.wait()
    load_srv.wait()
    pt[...] = (lax.broadcasted_iota(I32, (ROWS, ROWS), 0) == srv[...]).astype(BF16)
    ids_all[gi] = ids[...]
    for cp in load_h:
        cp.wait()

    pl.semaphore_wait(bar, len(peers))

    ycols = pl.ds(pl.multiple_of(y * YW, 128), YW)
    zcols = pl.ds(pl.multiple_of(ZB + z * ZW, ZW), ZW)
    cross_y, cross_z = [], []
    for h in range(2):
        for cols, cps in ((zcols, cross_z), (ycols, cross_y)):
            piece = h_all.at[h, gi, :, cols]
            cps.append(send(piece, piece, partner))
    pair = [send(h_all.at[h, gi], h_all.at[h, gi], other) for h in range(2)]
    idc = [send(ids_all.at[gi], ids_all.at[gi], (lax.rem(gi + k, GRPS), vi)) for k in range(1, GRPS)]

    gg = 2 * (1 - xh) + c
    fwd_y, fwd_z = [], []

    def forward(h):
        cross_z[h].wait_recv()
        piece = h_all.at[h, gg, :, zcols]
        fwd_z.append([send(piece, piece, p) for p in zs])
        cross_y[h].wait_recv()
        piece = h_all.at[h, gg, :, ycols]
        fwd_y.append([send(piece, piece, p) for p in ys])

    def share(h):
        cps = []
        for fwd, cols in ((fwd_y, pl.ds(0, ZB)), (fwd_z, pl.ds(ZB, NZ * ZW))):
            await_all(fwd[h])
            piece = h_all.at[h, gg, :, cols]
            cps.append(send(piece, piece, other))
        return cps

    def two_groups(part):
        return pl.ds(pl.multiple_of(part * GROWS, GROWS), GROWS)

    def logits(h, part):
        a = h_all[h, pl.ds(2 * part, 2)].reshape(GROWS, DS)
        lg[h, two_groups(part), :] = jnp.dot(a, w[...], preferred_element_type=F32)

    def student_stats(h, part):
        r = two_groups(part)
        l = lg[h, r, :]
        m = jnp.max(l, axis=1, keepdims=True)
        e = jnp.exp((l - m) * 0.5)
        lg[h, r, :] = e
        lane = lax.broadcasted_iota(I32, (GROWS, 128), 1)
        hard = jnp.sum(e * e, axis=1, keepdims=True)
        soft = jnp.sum(e, axis=1, keepdims=True)
        stc[h, r, :] = jnp.where(lane == 0, m, jnp.where(lane == 1, hard, soft))

    def turn_rows(h, part):
        cols = pl.ds(pl.multiple_of(h * HALF + part * GROWS, GROWS), GROWS)

        def step(i, _):
            s = pl.ds(pl.multiple_of(i * HW, HW), HW)
            ht[s, cols] = h_all[h, pl.ds(2 * part, 2), :, s].reshape(GROWS, HW).T
            return 0

        lax.fori_loop(0, HCH, step, 0)

    forward(0)
    load_w.wait()
    await_all(pair)
    logits(0, xh)
    load_t.wait()
    for q in range(GRPS):
        tst[q] = tv[:, q, :]
    t_all = tst[...].astype(F32)
    tm = jnp.max(jnp.max(t_all, axis=0), axis=1, keepdims=True)
    tsum = jnp.sum(jnp.sum(jnp.exp((t_all - tm[None]) * 0.5), axis=0), axis=1, keepdims=True)
    lse = jnp.broadcast_to(tm * 0.5 + jnp.log(tsum), (GROWS, 128)).T[0:1, :]
    none = jnp.full((1, GROWS), -1e30, F32)
    for j in range(GRPS):
        sta[0, 3 + j // 2 : 4 + j // 2, (j % 2) * GROWS : (j % 2 + 1) * GROWS] = jnp.where(gi == j, lse, none)
    forward(1)
    teach = []
    for k in range(1, GRPS):
        q = lax.rem(gi + k, GRPS)
        teach.append(send(tst.at[q], tall.at[gi], (q, vi)))
    tall[gi] = tst[gi]
    logits(1, xh)
    student_stats(0, xh)

    st = [sta, stb]
    st_x = [sta_x, stb_x]
    st_y = [sta_y, stb_y]
    st_z = [sta_z, stb_z]

    def stats_x(h):
        for j in range(2):
            s = slice(j * 128, (j + 1) * 128)
            st[h][0, 0:3, s] = stc[h, s, :].T[0:3, :]
        return [send(st[h].at[0], st_x[h].at[k], p) for k, p in enumerate([*xs, *xos, other])]

    def stats_y(h, cps):
        await_all(cps)
        put(st[h].at[2], merge([st[h][0], *[st_x[h][k] for k in range(2 * NX - 1)]]))
        return [send(st[h].at[2], st_y[h].at[k], p) for k, p in enumerate(ys)]

    def stats_z(h, cps):
        await_all(cps)
        put(st[h].at[3], merge([st[h][2], *[st_y[h][k] for k in range(NY - 1)]]))
        return [send(st[h].at[3], st_z[h].at[k], p) for k, p in enumerate(zs)]

    def stats_end(h, cps):
        await_all(cps)
        ms, hard, soft, *lse = merge([st[h][3], *[st_z[h][k] for k in range(NZ - 1)]])
        d = jnp.exp((st[h][0, 0:1, :] - ms) * 0.5)
        fin[0:1, :] = 32.0 * d / soft
        fin[1:2, :] = 16.0 * d * d / hard
        for j in range(2):
            s = slice(j * 128, (j + 1) * 128)
            fint[h, s, :] = fin[:, s].T
        return lse

    def turn_w(first, last):
        def step(i, _):
            s = pl.ds(pl.multiple_of(i * HW, HW), HW)
            wt[:, s] = w[s, :].T
            return 0

        lax.fori_loop(first, last, step, 0)

    def make_perm():
        i = lax.broadcasted_iota(I32, (HALF, 1), 0)
        i_c, hi, lo = lax.div(i, 128), lax.rem(lax.div(i, 32), 4), lax.rem(lax.div(i, 8), 4)
        i_z, i_b = lax.rem(lax.div(i, 2), 4), lax.rem(i, 2)
        col = lax.broadcasted_iota(I32, (HALF, HALF), 1)
        for p, (i_x, i_y) in enumerate(((hi, lo), (lo, hi))):
            r = (2 * lax.div(i_x, 2) + i_c) * HROWS + i_z * 16 + lax.rem(i_x, 2) * 8 + i_y * 2 + i_b
            perm[p] = (col == r).astype(BF16)

    fin[...] = jnp.zeros_like(fin)
    rowf[...] = jnp.zeros_like(rowf)
    shared = [share(0)]
    student_stats(1, xh)
    await_all(shared[0])
    logits(0, 1 - xh)
    student_stats(0, 1 - xh)
    m0 = stats_x(0)
    shared.append(share(1))
    await_all(shared[1])
    logits(1, 1 - xh)
    student_stats(1, 1 - xh)
    m1 = stats_x(1)
    m0 = stats_y(0, m0)
    make_perm()
    turn_w(0, 3)
    m0 = stats_z(0, m0)
    m1 = stats_y(1, m1)
    turn_w(3, HCH)

    await_all(teach)
    al[...] = lax.dot_general(
        pt[...], tall[...].reshape(ROWS, COLS), (((0,), (0,)), ((), ())), preferred_element_type=F32
    )
    await_all(idc)
    for j in range(GRPS):
        rowf[0:1, j * 128 : (j + 1) * 128] = ids_all[j].astype(F32)
    m1 = stats_z(1, m1)
    (lse,) = stats_end(0, m0)
    terms = 0.0
    for j in range(2):
        part = lse[j : j + 1, :]
        for k in range(3):
            term = part.astype(BF16).astype(F32)
            rowf[8 + k : 9 + k, j * HALF : (j + 1) * HALF] = term
            part = part - term
    terms = jnp.dot(rowf[8:16, :].astype(BF16), pt[...], preferred_element_type=F32)
    rowf[1:2, :] = terms[0:1] + terms[1:2] + terms[2:3]
    for j in range(4):
        s = slice(j * 128, (j + 1) * 128)
        rowt[s, :] = rowf[:, s].T

    first = (gi * (NX // 2 * NY * NZ) + vi) * COLS

    def teacher_part(h):
        def step(j, _):
            full = pl.ds(pl.multiple_of(j * GROWS + h * HROWS, HROWS), HROWS)
            f = rowt[full, :]
            col = lax.broadcasted_iota(I32, (HROWS, COLS), 1) + first
            hit = jnp.where(f[:, 0:1].astype(I32) == col, 16.0, 0.0)
            al[full, :] = 32.0 * jnp.exp(al[full, :] * 0.5 - f[:, 1:2]) + hit
            return 0

        lax.fori_loop(0, GRPS, step, 0)

    def grad(h):
        def step(j, _):
            r = pl.ds(pl.multiple_of(j * HROWS, HROWS), HROWS)
            full = pl.ds(pl.multiple_of(j * GROWS + h * HROWS, HROWS), HROWS)
            f = fint[h, r, :]
            e = lg[h, r, :]
            g[pl.ds(pl.multiple_of(h * HALF + j * HROWS, HROWS), HROWS), :] = (
                e * (f[:, 0:1] + e * f[:, 1:2]) - al[full, :]
            ).astype(BF16)
            return 0

        lax.fori_loop(0, GRPS, step, 0)
        for p in range(2):
            gp[p] = jnp.dot(perm[p], g[h * HALF : (h + 1) * HALF, :], preferred_element_type=F32).astype(BF16)

    pieces = [(p, i) for i in range(2) for p in range(2)]

    def partial(p, i, core):
        s = slice((2 * p + i) * SW, (2 * p + i + 1) * SW)
        return jnp.dot(gp[p, two_groups(core), :], wt[:, s], preferred_element_type=F32)

    def pair_stage(h):
        cps = {}
        for p, i in pieces:
            dsend[h, p, i] = partial(p, i, 1 - c).astype(BF16).reshape(4, 32, SW)
            cps[p, i] = send(dsend.at[h, p, i], drecv.at[h, p, i], other)
        return cps

    x_side = 2 * xh + 1 - xl
    y_side = y + 1 - 2 * lax.rem(y, 2)
    axes = [
        (x, ((3 - x, partner), (x_side, device(x_side, y, z, c))), y, ys),
        (y, ((3 - y, device(x, 3 - y, z, c)), (y_side, device(x, y_side, z, c))), x, xs),
    ]

    def chip_sum(h, p, i, k):
        return own[h, p, i, k] + drecv[h, p, i, k].astype(F32)

    def first_stage(h, cps):
        out = {}
        for p, i in pieces:
            own[h, p, i] = partial(p, i, c).reshape(4, 32, SW)
            cps[p, i].wait_recv()
            me, sides, _, _ = axes[p]
            place, to = sides[i]
            s1[h, p, i, 0] = chip_sum(h, p, i, place).astype(BF16)
            s1[h, p, i, 1] = chip_sum(h, p, i, lax.rem(me + 2, 4)).astype(BF16)
            out[p, i] = send(s1.at[h, p, i], r1.at[h, p, i], to)
        return out

    def first_stage_end(h, cps):
        out = {}
        for p, i in pieces:
            cps[p, i].wait_recv()
            place, to = axes[p][1][1 - i]
            s1b[h, p, i] = (chip_sum(h, p, i, place) + r1[h, p, i, 1].astype(F32)).astype(BF16)
            out[p, i] = send(s1b.at[h, p, i], r1b.at[h, p, i], to)
        return out

    def second_stage(h, cps):
        out = []
        for p in range(2):
            await_all([cps[p, 0], cps[p, 1]])
            me, _, me2, to = axes[p]
            t = [
                chip_sum(h, p, i, me) + (r1[h, p, i, 0].astype(F32) + r1b[h, p, i].astype(F32)) for i in range(2)
            ]
            for j in range(4):
                r = slice(j * 8, (j + 1) * 8)
                acc[h, p, j, :, :SW] = t[0][r]
                acc[h, p, j, :, SW:] = t[1][r]
                s2[h, p, j] = jnp.concatenate([t[0][r], t[1][r]], axis=0).astype(BF16)
            out.append([send(s2.at[h, p, lax.rem(me2 + k, 4)], r2.at[h, p, k - 1], d) for k, d in enumerate(to, 1)])
        return out

    base3 = 120
    s3f[:, 14:16, :] = jnp.zeros((NZ, 2, 512), F32)

    def third_copy(k, to):
        return pltpu.make_async_remote_copy(
            src_ref=s3.at[to],
            dst_ref=r3.at[k - 1],
            send_sem=ssem.at[base3 + k],
            recv_sem=rsem.at[base3 + k],
            device_id=device(x, y, to, c),
            device_id_type=MESH,
        )

    def third_stage(h, parts):
        for p, cps in enumerate(parts):
            await_all(cps)
            t = acc[h, p, axes[p][2]]
            u = r2[h, p, 0].astype(F32) + r2[h, p, 1].astype(F32) + r2[h, p, 2].astype(F32)
            base = p * CW
            acc3[:, base : base + SW] = t[:, : SW] + u[0:8]
            acc3[:, base + SW : base + CW] = t[:, SW :] + u[8:16]
        for j in range(4):
            for k in range(DS // 512):
                s3f[4 * h + j, 2 * k : 2 * k + 2, :] = acc3[2 * j : 2 * j + 2, k * 512 : (k + 1) * 512]
            s3[4 * h + j] = s3f[4 * h + j].astype(BF16)
        for k in range(1, NZ):
            to = lax.rem(z + k, NZ)

            @pl.when(lax.div(to, 4) == h)
            def _():
                third_copy(k, to).start()

    def third_end():
        for k in range(1, NZ):
            third_copy(k, lax.rem(z + k, NZ)).wait_recv()
        t = s3f[z]
        for k in range(NZ - 1):
            t = t + r3[k].astype(F32)
        for k in range(DS // 512):
            gh_out[:, k * 512 : (k + 1) * 512] = t[2 * k : 2 * k + 2, :]
        for k in range(1, NZ):
            third_copy(k, lax.rem(z + k, NZ)).wait_send()

    def head(first, last):
        def step(k, _):
            s = pl.ds(pl.multiple_of(k * HW, HW), HW)
            ghead_out[s, :] = jnp.dot(ht[s, :], g[...], preferred_element_type=F32).astype(BF16)
            return 0

        lax.fori_loop(first, last, step, 0)

    teacher_part(0)
    grad(0)
    m0 = pair_stage(0)
    teacher_part(1)
    m0 = first_stage(0, m0)
    stats_end(1, m1)
    grad(1)
    m1 = pair_stage(1)
    m1 = first_stage(1, m1)
    m0 = first_stage_end(0, m0)
    for h in range(2):
        turn_rows(h, xh)
    m0 = second_stage(0, m0)
    m1 = first_stage_end(1, m1)
    for h in range(2):
        turn_rows(h, 1 - xh)
    head(0, 2)
    m1 = second_stage(1, m1)
    third_stage(0, m0)
    head(2, HCH)
    third_stage(1, m1)
    third_end()

    for cp in started:
        cp.wait_send()


def write_out(sums, head, gh_out, ghead_out, sem):
    cps = [pltpu.make_async_copy(sums, gh_out, sem.at[HCH])]
    for k in range(HCH):
        s = pl.ds(k * HW, HW)
        cps.append(pltpu.make_async_copy(head.at[s], ghead_out.at[s], sem.at[k]))
    for cp in cps:
        cp.start()
    for cp in cps:
        cp.wait()


N_SEMS = 128


def body(hidden, token_ids, serving, head_weight, teacher_logits):
    vm = pltpu.VMEM
    sums, head = pl.pallas_call(
        kernel,
        out_shape=(
            vm((2, DS), F32),
            vm((DS, COLS), BF16),
        ),
        in_specs=[pl.BlockSpec(memory_space=pltpu.HBM)] * 5,
        out_specs=(pl.BlockSpec(memory_space=vm), pl.BlockSpec(memory_space=vm)),
        scratch_shapes=[
            vm((1, GROWS), I32),
            vm((1, ROWS), I32),
            vm((2, GRPS, HROWS, DS), BF16),
            vm((DS, COLS), BF16),
            vm((COLS, DS), BF16),
            vm((DS, ROWS), BF16),
            vm((GROWS, GRPS, COLS), BF16),
            vm((GRPS, GROWS, COLS), BF16),
            vm((GRPS, GROWS, COLS), BF16),
            vm((GRPS, 1, GROWS), I32),
            vm((ROWS, ROWS), BF16),
            vm((2, HALF, HALF), BF16),
            vm((2, HALF, COLS), F32),
            vm((ROWS, COLS), F32),
            vm((2, HALF, 128), F32),
            vm((4, 8, HALF), F32),
            vm((2 * NX - 1, 8, HALF), F32),
            vm((NY - 1, 8, HALF), F32),
            vm((NZ - 1, 8, HALF), F32),
            vm((4, 4, HALF), F32),
            vm((2 * NX - 1, 4, HALF), F32),
            vm((NY - 1, 4, HALF), F32),
            vm((NZ - 1, 4, HALF), F32),
            vm((128, HALF), F32),
            vm((2, HALF, 128), F32),
            vm((128, ROWS), F32),
            vm((ROWS, 128), F32),
            vm((ROWS, COLS), BF16),
            vm((2, HALF, COLS), BF16),
            vm((2, 2, 2, 4, 32, SW), F32),
            vm((2, 2, 2, 4, 32, SW), BF16),
            vm((2, 2, 2, 4, 32, SW), BF16),
            vm((2, 2, 2, 2, 32, SW), BF16),
            vm((2, 2, 2, 2, 32, SW), BF16),
            vm((2, 2, 2, 32, SW), BF16),
            vm((2, 2, 2, 32, SW), BF16),
            vm((2, 2, 4, 8, CW), F32),
            vm((2, 2, 4, 16, SW), BF16),
            vm((2, 2, 3, 16, SW), BF16),
            vm((8, DS), F32),
            vm((NZ, 16, 512), F32),
            vm((NZ, 16, 512), BF16),
            vm((NZ - 1, 16, 512), BF16),
            pltpu.SemaphoreType.DMA((N_SEMS,)),
            pltpu.SemaphoreType.DMA((N_SEMS,)),
            pltpu.SemaphoreType.DMA((6,)),
        ],
        compiler_params=pltpu.CompilerParams(
            collective_id=0, has_side_effects=True, vmem_limit_bytes=48 * 1024 * 1024
        ),
        name="distill_backward",
    )(*[
        pltpu.with_memory_space_constraint(a, pltpu.HBM)
        for a in (hidden, token_ids.reshape(1, GROWS), serving.reshape(1, ROWS), head_weight, teacher_logits)
    ])
    return pl.pallas_call(
        write_out,
        out_shape=(
            jax.ShapeDtypeStruct((2, DS), F32),
            jax.ShapeDtypeStruct((DS, COLS), BF16),
        ),
        in_specs=[pl.BlockSpec(memory_space=vm)] * 2,
        out_specs=(pl.BlockSpec(memory_space=pl.ANY), pl.BlockSpec(memory_space=pl.ANY)),
        scratch_shapes=[pltpu.SemaphoreType.DMA((1 + HCH,))],
        compiler_params=pltpu.CompilerParams(vmem_limit_bytes=1024 * 1024),
        name="write_out",
    )(sums, head)


def solution(mesh):
    placed = (P("grp", None), P("grp"), P(), P(None, ("grp", "vocab")), P("grp", None, "vocab"))
    return jax.shard_map(
        body,
        mesh=mesh,
        in_specs=placed,
        out_specs=(P(("grp", "vocab"), None), P(None, ("grp", "vocab"))),
        check_vma=False,
    )
```
